32 devices in a mesh: section: 4 (over x, core), dp: 4 (over z), mp: 2 (over y).
Axes of the slice: x: 2, y: 2, z: 4, core: 2. Of those that a mesh axis runs over, the one named last changes fastest.
Arguments:
- siglip_features: bfloat16 [2048, 1152], P('dp'), may hold values from -6 to 6
- convnext_features: bfloat16 [2048, 1536], P('dp'), may hold values from -6 to 6
- siglip_projection: bfloat16 [1152, 8192], P(None, ('section', 'mp')), may hold values from -0.125 to 0.125
- convnext_projection: bfloat16 [1536, 8192], P(None, ('section', 'mp')), may hold values from -0.125 to 0.125
- newline_embed: bfloat16 [8192], P(('section', 'mp')), may hold values from -6 to 6
- key_value_weight: bfloat16 [2048, 8192], P(None, ('section', 'mp')), may hold values from -0.0625 to 0.0625
- tile_rank: int32 [64, 1], replicated, may hold values from 0 to 3; in each aligned block of 16 rows (0 to 15, 16 to 31, ...) at most 8 rows name the same one
- row_end: int32 [64], replicated, may hold values 0 or 1
- key_value_grad: bfloat16 [4096, 2048], P('dp'), may hold values from -0.059814453 to 0.059814453
- newline_grad: bfloat16 [128, 2048], P('dp'), may hold values from -1.796875 to 1.796875
Outputs:
- siglip_weight_grad: float32 [1152, 8192], P('dp', ('section', 'mp'))
- convnext_weight_grad: float32 [1536, 8192], P('dp', ('section', 'mp'))
- key_value_weight_grad: float32 [2048, 8192], P('dp', ('section', 'mp'))
The draws below stay inside these ranges and needn't reach their ends.
Inputs may be any that keep to these rules, and one draw needn't show every extreme that they name: `tile_rank`: each aligned block of 16 tiles (the tiles of one index of dp) sends at most 8 tiles to one rank, and exactly 8 to some rank.
All inputs are finite; a program needn't handle non-finite values.
Results may differ from the reference program's by a relative error of at most 0.007.
Values may be sent and summed in bfloat16 or wider, within the bound.
A program may use at most 128 MiB of HBM per device.

```python
import math
import jax
import jax.numpy as jnp
import numpy as np
from jax import lax

D = 8192
SIG = 1152
CONV = 1536
TT = 32
TILE_DEV = 16
KV = 1024
CAP = 8
TILES = 64
SLOTS = 32
TOKENS = 2048
N_DP = 4


def plant(values, key, smallest, top_value):
    dims = values.shape
    place = [jax.random.randint(jax.random.fold_in(key, axis), (), 0, dims[axis]) for axis in range(len(dims))]
    values = values.at[tuple(place)].set(smallest)
    longest = dims.index(max(dims))
    place[longest] = (place[longest] + 1) % dims[longest]
    return values.at[tuple(place)].set(top_value)


def raised(drawn, rng, source, target, blocks, factor):
    def block_of(axis_at):
        return (jnp.arange(drawn.shape[axis_at]) // (drawn.shape[axis_at] // blocks)).reshape((-1,) + (1,) * (drawn.ndim - 1 - axis_at))

    first = jax.random.permutation(rng, blocks)[block_of(target)]
    far = (block_of(target) + blocks // 2) % blocks
    return jnp.where((block_of(source) == first) | (block_of(source) == far), factor * drawn, drawn)


def block_levels(key, dims, pieces, least, top_value):
    gain, own = 1.0, jax.random.fold_in(key, 6)
    for position, blocks in pieces:
        heights = jnp.exp(jax.random.uniform(jax.random.fold_in(own, position), (blocks,), jnp.float32, least / len(pieces), top_value / len(pieces)))
        gain = gain * jnp.repeat(heights, dims[position] // blocks).reshape([-1 if axis == position else 1 for axis in range(len(dims))])
    return gain


def assign_block(rng, own, number, rows, number_of, top, most, skew):
    sequence = jax.random.permutation(rng, number_of)
    packed, ordinary = portions_of(number_of, rows * top, most, skew, True), portions_of(number_of, rows * top, most, skew, False)
    places = jnp.arange(number_of)

    def named(sizes, rotation):
        used = int((sizes > 0).sum())
        fixed = max(1, used // 4)
        moved = fixed + (places - fixed + rotation * (used - fixed)) % max(1, number_of - fixed)
        return jnp.zeros((number_of,), jnp.int32).at[sequence[jnp.where(places < fixed, places, moved)]].set(jnp.asarray(sizes, jnp.int32))

    sizes = jnp.where(number % 4 == 0, named(packed, number // 4), named(ordinary, number - number // 4 - 1))
    mixed = jax.random.permutation(jax.random.fold_in(own, 3), number_of)
    giver, taker = mixed[0:number_of // 2 * 2:2], mixed[1:number_of // 2 * 2:2]
    slack = jnp.minimum(sizes[giver] - 1, most - sizes[taker]) // 2
    slack = jnp.where((giver == sequence[0]) | (taker == sequence[0]) | (sizes[taker] == 0), 0, jnp.maximum(slack, 0))
    moved = jax.random.randint(jax.random.fold_in(own, 4), (number_of // 2,), 0, 1 << 20) % (slack + 1)
    sizes = sizes.at[giver].add(-moved).at[taker].add(moved)
    members = jnp.searchsorted(jnp.cumsum(sizes), jnp.arange(rows * top), side="right").astype(jnp.int32)
    table = members.reshape(top, rows).T
    table = table[jax.random.permutation(jax.random.fold_in(own, 1), rows)]
    rotation = jax.random.randint(jax.random.fold_in(own, 2), (rows, 1), 0, top)
    return jnp.take_along_axis(table, (jnp.arange(top)[None, :] + rotation) % top, axis=1)


def portions_of(count, total, limit, slope, full):
    weights = [(1 << 20) // math.isqrt(grade ** slope) + 1 for grade in range(1, count + 1)]
    largest = limit if full else min(limit, max(-(-total // count), total * weights[0] // sum(weights)))
    least = 1 if total - largest >= count - 1 else 0
    holding, surplus = [largest] + [least] * (count - 1), total - largest - least * (count - 1)
    while surplus > 0:
        free = [i for i in range(1, count) if holding[i] < largest] or [i for i in range(1, count) if holding[i] < limit]
        mass, left = sum([weights[i] for i in free]), surplus
        for i in free:
            addition = min(limit - holding[i], max(1, left * weights[i] // mass), surplus)
            holding[i] = holding[i] + addition
            surplus = surplus - addition
    return np.array(holding)


def noise(key, extent, deviation, most, cuts=(), kind=jnp.bfloat16):
    level = block_levels(key, extent, cuts, -0.22, 0.18) if cuts else 1.0
    values = jax.random.normal(key, extent, jnp.float32) * deviation * level
    return jnp.minimum(jnp.maximum(values, -most), most).astype(kind)


def bell_draw_with(key, shape, width, reach, pieces, heavy, kind=jnp.bfloat16):
    drawn = width * jax.random.normal(key, shape, jnp.float32)
    if pieces:
        drawn = drawn * block_levels(key, shape, pieces, -0.22, 0.18)
    return jnp.clip(raised(drawn, jax.random.fold_in(key, 3), *heavy), -reach, reach).astype(kind)


def setup_inputs(seed: int = 0) -> dict:
    seeds = jax.random.split(jax.random.key(seed), 11)
    siglip_features = bell_draw_with(seeds[0], (TOKENS, SIG), 1.0, 6.0, ((0, 4),), (0, 1, 4, 2.0))
    convnext_features = bell_draw_with(seeds[1], (TOKENS, CONV), 1.0, 6.0, ((0, 4),), (0, 1, 4, 2.0))
    siglip_projection = noise(seeds[2], (SIG, D), (SIG + CONV) ** -0.5, 0.125, ((1, 8),))
    convnext_projection = noise(seeds[3], (CONV, D), (SIG + CONV) ** -0.5, 0.125, ((1, 8),))
    newline_embed = noise(seeds[4], (D,), 1.0, 6.0, ((0, 8),))
    key_value_weight = noise(seeds[5], (2 * KV, D), D ** -0.5, 0.0625, ((1, 8),))
    tile_rank_keys = jax.random.split(jax.random.fold_in(seeds[6], 1), TILES // TILE_DEV)
    tile_rank_turns = jax.random.permutation(jax.random.fold_in(seeds[6], 3), TILES // TILE_DEV)
    tile_rank = jax.vmap(lambda own, number: assign_block(jax.random.fold_in(seeds[6], 2), own, number, TILE_DEV, N_DP, 1, CAP, 2))(tile_rank_keys, tile_rank_turns).reshape((TILES, 1))
    row_end = plant((jax.random.randint(seeds[7], (TILES,), 0, 3) < 1).astype(jnp.int32), jax.random.fold_in(seeds[7], 1), 0, 1)
    key_value_grad = bell_draw_with(seeds[8], (N_DP * SLOTS * TT, 2 * KV), 0.01, 0.059814453, ((0, 4),), (0, 1, 4, 2.0))
    newline_grad = noise(seeds[9], (N_DP * SLOTS, 2 * KV), 0.3, 1.796875, ((0, 4),))
    return dict(siglip_features=siglip_features, convnext_features=convnext_features, siglip_projection=siglip_projection, convnext_projection=convnext_projection, newline_embed=newline_embed, key_value_weight=key_value_weight, tile_rank=tile_rank, row_end=row_end, key_value_grad=key_value_grad, newline_grad=newline_grad)


epsilon = 1e-06

def tile_slots(tile_rank):
    dest_rank = tile_rank[:, 0].astype(jnp.int32)
    tile_count = dest_rank.shape[0]
    per_device = tile_count // N_DP
    onehot = (dest_rank[:, None] == jnp.arange(N_DP, dtype=jnp.int32)[None, :]).astype(jnp.int32)
    blocks = onehot.reshape(N_DP, per_device, N_DP)
    before = jnp.cumsum(blocks, axis=1) - blocks
    slot_place = lax.optimization_barrier(jnp.sum(before * blocks, axis=2)).reshape(tile_count).astype(jnp.int32)
    source = (jnp.arange(tile_count, dtype=jnp.int32) // per_device).astype(jnp.int32)
    return ((dest_rank * N_DP + source) * CAP + slot_place).astype(jnp.int32)

def reference(siglip_features, convnext_features, siglip_projection, convnext_projection, newline_embed, key_value_weight, tile_rank, row_end, key_value_grad, newline_grad):
    slot_index = tile_slots(tile_rank)
    projected = (jnp.dot(siglip_features, siglip_projection, preferred_element_type=jnp.float32) + jnp.dot(convnext_features, convnext_projection, preferred_element_type=jnp.float32)).astype(jnp.bfloat16)
    proj_values = projected.astype(jnp.float32)
    inverse_rms = lax.rsqrt(lax.optimization_barrier(jnp.mean(proj_values * proj_values, axis=1, keepdims=True)) + epsilon)
    normed = (proj_values * inverse_rms).astype(jnp.bfloat16)
    line_vector = newline_embed.astype(jnp.float32)
    line_normed = (line_vector * lax.rsqrt(jnp.mean(line_vector * line_vector) + epsilon)).astype(jnp.bfloat16)
    tile_grads = key_value_grad.reshape(N_DP * SLOTS, TT, 2 * KV)[slot_index].reshape(TILES * TT, 2 * KV)
    kv_term = jnp.dot(tile_grads.T, normed, preferred_element_type=jnp.float32)
    line_rows = newline_grad[slot_index].astype(jnp.float32) * row_end.astype(jnp.float32)[:, None]
    line_total = lax.optimization_barrier(jnp.sum(line_rows, axis=0))
    key_value_weight_grad = kv_term + line_total[:, None] * line_normed.astype(jnp.float32)[None, :]
    normed_grad = jnp.dot(tile_grads, key_value_weight, preferred_element_type=jnp.float32).astype(jnp.bfloat16)
    grad_values = normed_grad.astype(jnp.float32)
    products = lax.optimization_barrier(jnp.sum(grad_values * proj_values, axis=1, keepdims=True))
    projected_grad = (inverse_rms * grad_values - inverse_rms ** 3 * proj_values * products / D).astype(jnp.bfloat16)
    siglip_weight_grad = jnp.dot(siglip_features.T, projected_grad, preferred_element_type=jnp.float32)
    convnext_weight_grad = jnp.dot(convnext_features.T, projected_grad, preferred_element_type=jnp.float32)
    return (siglip_weight_grad, convnext_weight_grad, key_value_weight_grad)
```

```python
import jax
import jax.numpy as jnp
from jax import lax
from jax.sharding import PartitionSpec as P

D = 8192


epsilon = 1e-06


def tile_places(tile_rank, groups):
    dest_rank = tile_rank[:, 0]
    tile_count = dest_rank.shape[0]
    per_device = tile_count // groups
    onehot = (dest_rank[:, None] == jnp.arange(groups, dtype=jnp.int32)[None, :]).astype(jnp.int32)
    blocks = onehot.reshape(groups, per_device, groups)
    before = jnp.cumsum(blocks, axis=1) - blocks
    slot_place = jnp.sum(before * blocks, axis=2).reshape(tile_count)
    source = jnp.arange(tile_count, dtype=jnp.int32) // per_device
    return (dest_rank, source, slot_place)


def row_norms(squares):
    return lax.psum((squares[0], squares[1]), ("section", "mp"))


def row_products(products):
    return lax.psum(products, ("section", "mp"))


def norm_backward(inverse_rms, grad_values, proj_values):
    products = row_products(jnp.sum(grad_values * proj_values, axis=1))[:, None]
    return (inverse_rms * grad_values - inverse_rms**3 * proj_values * products / D).astype(
        jnp.bfloat16
    )


def local_reducing(
    siglip_features,
    convnext_features,
    siglip_projection,
    convnext_projection,
    newline_embed,
    key_value_weight,
    tile_rank,
    row_end,
    key_value_grad,
    newline_grad,
):
    groups = lax.axis_size("dp")
    my_rank = lax.axis_index("dp")
    dest_rank, source, slot_place = tile_places(tile_rank, groups)
    per_device = dest_rank.shape[0] // groups
    capacity = 2 * per_device // groups
    row_count = siglip_features.shape[0]
    tile_rows = row_count // per_device
    share = siglip_projection.shape[1]
    mine_dest = lax.dynamic_slice_in_dim(dest_rank, my_rank * per_device, per_device)
    mine_place = lax.dynamic_slice_in_dim(slot_place, my_rank * per_device, per_device)
    rank_ids = jnp.arange(groups, dtype=jnp.int32)[:, None, None]
    place_ids = jnp.arange(capacity, dtype=jnp.int32)[None, :, None]
    select = (
        (mine_dest[None, None, :] == rank_ids) & (mine_place[None, None, :] == place_ids)
    ).astype(jnp.bfloat16)
    projected = (
        jnp.dot(siglip_features, siglip_projection, preferred_element_type=jnp.float32)
        + jnp.dot(convnext_features, convnext_projection, preferred_element_type=jnp.float32)
    ).astype(jnp.bfloat16)
    line_vector = newline_embed.astype(jnp.float32)
    line_square = jnp.sum(line_vector * line_vector)
    outgoing = jnp.einsum(
        "gcj,jtx->gctx",
        select,
        projected.reshape(per_device, tile_rows, share),
        preferred_element_type=jnp.float32,
    ).astype(jnp.bfloat16)
    outgoing = outgoing.reshape(groups, capacity * tile_rows, share)
    received = lax.all_to_all(outgoing, "dp", split_axis=0, concat_axis=0, tiled=True).reshape(
        groups * capacity * tile_rows, share
    )
    recv_values = received.astype(jnp.float32)
    statistic = row_norms((jnp.sum(recv_values * recv_values, axis=1), line_square))
    recv_inverse = lax.rsqrt(statistic[0] / D + epsilon)[:, None]
    line_total_sq = statistic[1]
    normed = (recv_values * recv_inverse).astype(jnp.bfloat16)
    line_normed = (line_vector * lax.rsqrt(line_total_sq / D + epsilon)).astype(jnp.bfloat16)
    slot_global = source * capacity + slot_place
    line_live = (dest_rank == my_rank) & (row_end == 1)
    slot_ids = jnp.arange(groups * capacity, dtype=jnp.int32)[None, :]
    newline_mask = jnp.sum(
        ((slot_global[:, None] == slot_ids) & line_live[:, None]).astype(jnp.int32), axis=0
    )
    line_total = jnp.dot(
        newline_mask.astype(jnp.bfloat16)[None, :], newline_grad, preferred_element_type=jnp.float32
    )[0]
    kv_term = lax.dot_general(
        key_value_grad, normed, (((0,), (0,)), ((), ())), preferred_element_type=jnp.float32
    )
    kv_term = kv_term + line_total[:, None] * line_normed.astype(jnp.float32)[None, :]
    normed_grad = jnp.dot(
        key_value_grad, key_value_weight, preferred_element_type=jnp.float32
    ).astype(jnp.bfloat16)
    returning = norm_backward(recv_inverse, normed_grad.astype(jnp.float32), recv_values)
    returned = lax.all_to_all(
        returning.reshape(groups, capacity * tile_rows, share),
        "dp",
        split_axis=0,
        concat_axis=0,
        tiled=True,
    )
    tile_back = jnp.einsum(
        "gcj,gctx->jtx",
        select,
        returned.reshape(groups, capacity, tile_rows, share),
        preferred_element_type=jnp.float32,
    ).reshape(row_count, share)
    projected_grad = tile_back.astype(jnp.bfloat16)
    contract = (((0,), (0,)), ((), ()))
    siglip_term = lax.dot_general(
        siglip_features, projected_grad, contract, preferred_element_type=jnp.float32
    )
    convnext_term = lax.dot_general(
        convnext_features, projected_grad, contract, preferred_element_type=jnp.float32
    )
    siglip_result, convnext_result, kv_result = (
        lax.psum_scatter(siglip_term, "dp", scatter_dimension=0, tiled=True),
        lax.psum_scatter(convnext_term, "dp", scatter_dimension=0, tiled=True),
        lax.psum_scatter(kv_term, "dp", scatter_dimension=0, tiled=True),
    )
    return (siglip_result, convnext_result, kv_result)


def local_gathering(
    siglip_features,
    convnext_features,
    siglip_projection,
    convnext_projection,
    newline_embed,
    key_value_weight,
    tile_rank,
    row_end,
    key_value_grad,
    newline_grad,
):
    groups = lax.axis_size("dp")
    mates = lax.axis_size("section") * lax.axis_size("mp")
    my_rank = lax.axis_index("dp")
    me = lax.axis_index("section") * lax.axis_size("mp") + lax.axis_index("mp")
    dest_rank, source, slot_place = tile_places(tile_rank, groups)
    per_device = dest_rank.shape[0] // groups
    capacity = 2 * per_device // groups
    row_count, sig = siglip_features.shape
    conv = convnext_features.shape[1]
    tile_rows = row_count // per_device
    part = tile_rows // mates
    kv = key_value_grad.shape[1]
    everyone = ("dp", "section", "mp")

    def my_rows(x, tiles):
        x = x.reshape(tiles, tile_rows, x.shape[1])
        return lax.dynamic_slice_in_dim(x, me * part, part, axis=1)

    features = jnp.concatenate([siglip_features, convnext_features], axis=1)
    features = my_rows(features, per_device).reshape(per_device * part, sig + conv)
    features = lax.all_gather(features, everyone, axis=0, tiled=True)

    slots = my_rows(key_value_grad, groups * capacity).reshape(groups, capacity * part * kv)
    slots = lax.all_to_all(slots, "dp", split_axis=0, concat_axis=0, tiled=True)
    mine_dest = lax.dynamic_slice_in_dim(dest_rank, my_rank * per_device, per_device)
    mine_place = lax.dynamic_slice_in_dim(slot_place, my_rank * per_device, per_device)
    wanted = mine_dest * capacity + mine_place
    select = (wanted[:, None] == jnp.arange(groups * capacity, dtype=jnp.int32)[None, :]).astype(
        jnp.bfloat16
    )
    grads = jnp.dot(
        select, slots.reshape(groups * capacity, part * kv), preferred_element_type=jnp.float32
    ).astype(jnp.bfloat16)
    grads = lax.all_gather(grads.reshape(per_device * part, kv), everyone, axis=0, tiled=True)

    slot_global = source * capacity + slot_place
    line_live = (dest_rank == my_rank) & (row_end == 1)
    slot_ids = jnp.arange(groups * capacity, dtype=jnp.int32)[None, :]
    newline_mask = jnp.sum(
        ((slot_global[:, None] == slot_ids) & line_live[:, None]).astype(jnp.int32), axis=0
    )
    line_total = jnp.dot(
        newline_mask.astype(jnp.bfloat16)[None, :], newline_grad, preferred_element_type=jnp.float32
    )[0]
    line_total = lax.psum_scatter(line_total, "dp", scatter_dimension=0, tiled=True)
    line_vector = newline_embed.astype(jnp.float32)
    line_square = jnp.sum(line_vector * line_vector)

    projected = (
        jnp.dot(features[:, :sig], siglip_projection, preferred_element_type=jnp.float32)
        + jnp.dot(features[:, sig:], convnext_projection, preferred_element_type=jnp.float32)
    ).astype(jnp.bfloat16)
    proj_values = projected.astype(jnp.float32)
    normed_grad = jnp.dot(grads, key_value_weight, preferred_element_type=jnp.float32).astype(
        jnp.bfloat16
    )
    grad_values = normed_grad.astype(jnp.float32)
    squares = jnp.sum(proj_values * proj_values, axis=1)
    products = jnp.sum(grad_values * proj_values, axis=1)
    squares, products, line_square = lax.psum((squares, products, line_square), ("section", "mp"))
    inverse = lax.rsqrt(squares / D + epsilon)[:, None]
    normed = (proj_values * inverse).astype(jnp.bfloat16)
    line_normed = (line_vector * lax.rsqrt(line_square / D + epsilon)).astype(jnp.bfloat16)
    projected_grad = (
        inverse * grad_values - inverse**3 * proj_values * products[:, None] / D
    ).astype(jnp.bfloat16)

    def block(x, first, width):
        return lax.dynamic_slice_in_dim(x, first + my_rank * (width // groups), width // groups, 1)

    def contract(a, b):
        return lax.dot_general(a, b, (((0,), (0,)), ((), ())), preferred_element_type=jnp.float32)

    siglip_result = contract(block(features, 0, sig), projected_grad)
    convnext_result = contract(block(features, sig, conv), projected_grad)
    kv_result = contract(block(grads, 0, kv), normed)
    kv_result = kv_result + line_total[:, None] * line_normed.astype(jnp.float32)[None, :]
    return (siglip_result, convnext_result, kv_result)


GATHER_LIMIT = 40 * 2**20


def local(*args):
    rows = lax.axis_size("dp") * args[0].shape[0]
    width = args[0].shape[1] + args[1].shape[1] + args[8].shape[1]
    if 2 * rows * width <= GATHER_LIMIT:
        return local_gathering(*args)
    return local_reducing(*args)


def solution(mesh):
    in_specs = (
        P("dp", None),
        P("dp", None),
        P(None, ("section", "mp")),
        P(None, ("section", "mp")),
        P(("section", "mp")),
        P(None, ("section", "mp")),
        P(),
        P(),
        P("dp", None),
        P("dp", None),
    )
    out_specs = (P("dp", ("section", "mp")), P("dp", ("section", "mp")), P("dp", ("section", "mp")))
    return jax.shard_map(local, mesh=mesh, in_specs=in_specs, out_specs=out_specs, check_vma=False)
```

```python
import functools

import jax
import jax.numpy as jnp
from jax import lax
from jax.experimental import pallas as pl
from jax.experimental.pallas import tpu as pltpu
from jax.sharding import PartitionSpec as P

D = 8192


epsilon = 1e-06


def tile_places(tile_rank, groups):
    dest_rank = tile_rank[:, 0]
    tile_count = dest_rank.shape[0]
    per_device = tile_count // groups
    onehot = (dest_rank[:, None] == jnp.arange(groups, dtype=jnp.int32)[None, :]).astype(jnp.int32)
    blocks = onehot.reshape(groups, per_device, groups)
    before = jnp.cumsum(blocks, axis=1) - blocks
    slot_place = jnp.sum(before * blocks, axis=2).reshape(tile_count)
    source = jnp.arange(tile_count, dtype=jnp.int32) // per_device
    return (dest_rank, source, slot_place)


def row_norms(squares):
    return lax.psum((squares[0], squares[1]), ("section", "mp"))


def row_products(products):
    return lax.psum(products, ("section", "mp"))


def norm_backward(inverse_rms, grad_values, proj_values):
    products = row_products(jnp.sum(grad_values * proj_values, axis=1))[:, None]
    return (inverse_rms * grad_values - inverse_rms**3 * proj_values * products / D).astype(
        jnp.bfloat16
    )


def local_reducing(
    siglip_features,
    convnext_features,
    siglip_projection,
    convnext_projection,
    newline_embed,
    key_value_weight,
    tile_rank,
    row_end,
    key_value_grad,
    newline_grad,
):
    groups = lax.axis_size("dp")
    my_rank = lax.axis_index("dp")
    dest_rank, source, slot_place = tile_places(tile_rank, groups)
    per_device = dest_rank.shape[0] // groups
    capacity = 2 * per_device // groups
    row_count = siglip_features.shape[0]
    tile_rows = row_count // per_device
    share = siglip_projection.shape[1]
    mine_dest = lax.dynamic_slice_in_dim(dest_rank, my_rank * per_device, per_device)
    mine_place = lax.dynamic_slice_in_dim(slot_place, my_rank * per_device, per_device)
    rank_ids = jnp.arange(groups, dtype=jnp.int32)[:, None, None]
    place_ids = jnp.arange(capacity, dtype=jnp.int32)[None, :, None]
    select = (
        (mine_dest[None, None, :] == rank_ids) & (mine_place[None, None, :] == place_ids)
    ).astype(jnp.bfloat16)
    projected = (
        jnp.dot(siglip_features, siglip_projection, preferred_element_type=jnp.float32)
        + jnp.dot(convnext_features, convnext_projection, preferred_element_type=jnp.float32)
    ).astype(jnp.bfloat16)
    line_vector = newline_embed.astype(jnp.float32)
    line_square = jnp.sum(line_vector * line_vector)
    outgoing = jnp.einsum(
        "gcj,jtx->gctx",
        select,
        projected.reshape(per_device, tile_rows, share),
        preferred_element_type=jnp.float32,
    ).astype(jnp.bfloat16)
    outgoing = outgoing.reshape(groups, capacity * tile_rows, share)
    received = lax.all_to_all(outgoing, "dp", split_axis=0, concat_axis=0, tiled=True).reshape(
        groups * capacity * tile_rows, share
    )
    recv_values = received.astype(jnp.float32)
    statistic = row_norms((jnp.sum(recv_values * recv_values, axis=1), line_square))
    recv_inverse = lax.rsqrt(statistic[0] / D + epsilon)[:, None]
    line_total_sq = statistic[1]
    normed = (recv_values * recv_inverse).astype(jnp.bfloat16)
    line_normed = (line_vector * lax.rsqrt(line_total_sq / D + epsilon)).astype(jnp.bfloat16)
    slot_global = source * capacity + slot_place
    line_live = (dest_rank == my_rank) & (row_end == 1)
    slot_ids = jnp.arange(groups * capacity, dtype=jnp.int32)[None, :]
    newline_mask = jnp.sum(
        ((slot_global[:, None] == slot_ids) & line_live[:, None]).astype(jnp.int32), axis=0
    )
    line_total = jnp.dot(
        newline_mask.astype(jnp.bfloat16)[None, :], newline_grad, preferred_element_type=jnp.float32
    )[0]
    kv_term = lax.dot_general(
        key_value_grad, normed, (((0,), (0,)), ((), ())), preferred_element_type=jnp.float32
    )
    kv_term = kv_term + line_total[:, None] * line_normed.astype(jnp.float32)[None, :]
    normed_grad = jnp.dot(
        key_value_grad, key_value_weight, preferred_element_type=jnp.float32
    ).astype(jnp.bfloat16)
    returning = norm_backward(recv_inverse, normed_grad.astype(jnp.float32), recv_values)
    returned = lax.all_to_all(
        returning.reshape(groups, capacity * tile_rows, share),
        "dp",
        split_axis=0,
        concat_axis=0,
        tiled=True,
    )
    tile_back = jnp.einsum(
        "gcj,gctx->jtx",
        select,
        returned.reshape(groups, capacity, tile_rows, share),
        preferred_element_type=jnp.float32,
    ).reshape(row_count, share)
    projected_grad = tile_back.astype(jnp.bfloat16)
    contract = (((0,), (0,)), ((), ()))
    siglip_term = lax.dot_general(
        siglip_features, projected_grad, contract, preferred_element_type=jnp.float32
    )
    convnext_term = lax.dot_general(
        convnext_features, projected_grad, contract, preferred_element_type=jnp.float32
    )
    siglip_result, convnext_result, kv_result = (
        lax.psum_scatter(siglip_term, "dp", scatter_dimension=0, tiled=True),
        lax.psum_scatter(convnext_term, "dp", scatter_dimension=0, tiled=True),
        lax.psum_scatter(kv_term, "dp", scatter_dimension=0, tiled=True),
    )
    return (siglip_result, convnext_result, kv_result)


FROM_X, FROM_Y, FROM_CORE, HALF_X, HALF_Y, CORE_X, CORE_Y, CORE_HX, CORE_HY = range(9)
MESH = pl.DeviceIdType.MESH


def gather_kernel(
    groups,
    sig_ref,
    conv_ref,
    sig_w,
    conv_w,
    kv_w,
    kv_grad,
    select,
    f_out,
    g_out,
    proj,
    ngrad,
    f,
    g,
    slots,
    mine,
    local_sem,
    slot_send,
    slot_recv,
    line_send,
    line_recv,
    send,
    recv,
    out_sem,
):
    section = lax.axis_index("section")
    z = lax.axis_index("dp")
    y = lax.axis_index("mp")
    rows, sig = sig_ref.shape
    conv = conv_ref.shape[1]
    kv = kv_grad.shape[1]
    part = rows // 8
    wide = kv // 8
    slot_rows = kv_grad.shape[0] // groups
    x_section = lax.rem(section + 2, 4)
    core_section = section + 1 - 2 * lax.rem(section, 2)
    at_x = (x_section, z, y)
    at_y = (section, z, 1 - y)
    at_core = (core_section, z, y)

    def number(sec, yy):
        return sec * 2 + yy

    me = number(section, y)
    from_x, from_y = number(x_section, y), number(section, 1 - y)
    diag = number(x_section, 1 - y)
    core = [
        number(core_section, y),
        number(lax.rem(core_section + 2, 4), y),
        number(core_section, 1 - y),
        number(lax.rem(core_section + 2, 4), 1 - y),
    ]

    def peer(k):
        return (section, lax.rem(z + k, groups), y)

    barrier = pltpu.get_barrier_semaphore()
    for device in [peer(k) for k in range(1, groups)] + [at_x, at_y, at_core]:
        pl.semaphore_signal(barrier, inc=1, device_id=device, device_id_type=MESH)
    pl.semaphore_wait(barrier, groups + 2)

    def shard(is_f, q, m, half=None):
        if is_f:
            first, count = q * rows + m * part, part
        else:
            first, count = q * rows, rows
        if half is not None:
            count //= 2
            first = first + half * count
        first = pl.multiple_of(first, 32)
        if is_f:
            return f.at[pl.ds(first, count), :]
        return g.at[pl.ds(first, count), pl.ds(pl.multiple_of(m * wide, 128), wide)]

    def remote(ref, device, ss, rs, dst=None):
        return pltpu.make_async_remote_copy(
            src_ref=ref,
            dst_ref=ref if dst is None else dst,
            send_sem=ss,
            recv_sem=rs,
            device_id=device,
            device_id_type=MESH,
        )

    sent = []
    own = pl.ds(pl.multiple_of(z * rows, rows), rows)
    my_cols = pl.ds(pl.multiple_of(me * wide, 128), wide)

    def slot_block(q):
        return pl.ds(pl.multiple_of(q * slot_rows, slot_rows), slot_rows)

    locals_ = [
        pltpu.make_async_copy(sig_ref, f.at[own, pl.ds(0, sig)], local_sem.at[0]),
        pltpu.make_async_copy(conv_ref, f.at[own, pl.ds(sig, conv)], local_sem.at[1]),
        pltpu.make_async_copy(
            kv_grad.at[slot_block(z), my_cols], slots.at[slot_block(z), :], local_sem.at[2]
        ),
    ]
    for copy in locals_:
        copy.start()
    for k in range(1, groups):
        copy = remote(
            kv_grad.at[slot_block(lax.rem(z + k, groups)), my_cols],
            peer(k),
            slot_send.at[k],
            slot_recv.at[k],
            slots.at[slot_block(z), :],
        )
        copy.start()
        sent.append(copy)
    for copy in locals_:
        copy.wait()

    def line(is_f):
        for k in range(1, groups):
            at = (0 if is_f else groups) + k
            copy = remote(shard(is_f, z, me), peer(k), line_send.at[at], line_recv.at[at])
            copy.start()
            sent.append(copy)

    line(True)
    step = 256

    def compute(is_f, q):
        block = pl.ds(pl.multiple_of(q * rows, rows), rows)

        @pl.loop(0, proj.shape[1] // step)
        def _(n):
            cols = pl.ds(pl.multiple_of(n * step, step), step)
            if is_f:
                total = jnp.dot(
                    f[block, :sig], sig_w[:, cols], preferred_element_type=jnp.float32
                ) + jnp.dot(f[block, sig:], conv_w[:, cols], preferred_element_type=jnp.float32)
                proj[block, cols] = total.astype(jnp.bfloat16)
            else:
                total = jnp.dot(g[block, :], kv_w[:, cols], preferred_element_type=jnp.float32)
                ngrad[block, cols] = total.astype(jnp.bfloat16)

    written = []

    def put(is_f, k):
        q = lax.rem(z - k + groups, groups)
        block = pl.ds(pl.multiple_of(q * rows, rows), rows)
        if is_f:
            copy = pltpu.make_async_copy(f.at[block, :], f_out.at[block, :], out_sem.at[k])
        else:
            copy = pltpu.make_async_copy(g.at[block, :], g_out.at[block, :], out_sem.at[groups + k])
        copy.start()
        written.append(copy)

    put(True, 0)
    compute(True, z)

    for k in range(1, groups):
        q = lax.rem(z - k + groups, groups)
        ref = slots.at[slot_block(q), :]
        remote(ref, peer(k), slot_send.at[k], slot_recv.at[k]).wait_recv()
    mine[...] = jnp.dot(select[...], slots[...], preferred_element_type=jnp.float32).astype(
        jnp.bfloat16
    )
    copy = pltpu.make_async_copy(mine, shard(False, z, me), local_sem.at[3])
    copy.start()
    copy.wait()
    line(False)

    items = [(False, 0), (True, 1), (True, 3), (True, 2), (False, 1), (False, 3), (False, 2)]

    def go(i, ref, device, kind):
        copy = remote(ref, device, send.at[i, kind], recv.at[i, kind])
        copy.start()
        sent.append(copy)

    def take(i, ref, kind):
        remote(ref, at_core, send.at[i, kind], recv.at[i, kind]).wait_recv()

    def owner(i):
        is_f, k = items[i]
        return is_f, lax.rem(z - k + groups, groups)

    def spread(i):
        is_f, q = owner(i)
        k = items[i][1]
        ref = shard(is_f, q, me)
        if k:
            at = (0 if is_f else groups) + k
            remote(ref, at_core, line_send.at[at], line_recv.at[at]).wait_recv()
        go(i, ref, at_x, FROM_X)
        go(i, ref, at_y, FROM_Y)
        go(i, ref, at_core, FROM_CORE)

    def forward(i):
        is_f, q = owner(i)
        take(i, shard(is_f, q, from_x), FROM_X)
        go(i, shard(is_f, q, from_x, 0), at_y, HALF_Y)
        go(i, shard(is_f, q, from_x), at_core, CORE_X)
        take(i, shard(is_f, q, from_y), FROM_Y)
        go(i, shard(is_f, q, from_y, 1), at_x, HALF_X)
        go(i, shard(is_f, q, from_y), at_core, CORE_Y)

    def halves(i):
        is_f, q = owner(i)
        take(i, shard(is_f, q, diag, 0), HALF_Y)
        go(i, shard(is_f, q, diag, 0), at_core, CORE_HY)
        take(i, shard(is_f, q, diag, 1), HALF_X)
        go(i, shard(is_f, q, diag, 1), at_core, CORE_HX)

    def finish(i):
        is_f, q = owner(i)
        take(i, shard(is_f, q, core[0]), FROM_CORE)
        take(i, shard(is_f, q, core[1]), CORE_X)
        take(i, shard(is_f, q, core[2]), CORE_Y)
        take(i, shard(is_f, q, core[3], 0), CORE_HY)
        take(i, shard(is_f, q, core[3], 1), CORE_HX)
        put(is_f, items[i][1])
        compute(is_f, q)

    count = len(items)
    for t in range(count + 3):
        for lag, stage in enumerate((spread, forward, halves, finish)):
            if 0 <= t - lag < count:
                stage(t - lag)
    for copy in sent:
        copy.wait_send()
    for copy in written:
        copy.wait()


def gather_and_project(sig_x, conv_x, sig_w, conv_w, kv_w, kv_grad, select):
    groups = lax.axis_size("dp")
    rows, sig = sig_x.shape
    conv = conv_x.shape[1]
    kv = kv_grad.shape[1]
    share = sig_w.shape[1]
    everything = groups * rows
    half = jnp.bfloat16
    hbm = pl.BlockSpec(memory_space=pl.ANY)
    vmem = pl.BlockSpec(memory_space=pltpu.VMEM)
    dma = pltpu.SemaphoreType.DMA
    return pl.pallas_call(
        functools.partial(gather_kernel, groups),
        out_shape=(
            jax.ShapeDtypeStruct((everything, sig + conv), half),
            jax.ShapeDtypeStruct((everything, kv), half),
            jax.ShapeDtypeStruct((everything, share), half),
            jax.ShapeDtypeStruct((everything, share), half),
        ),
        in_specs=[hbm, hbm, vmem, vmem, vmem, hbm, vmem],
        out_specs=(hbm, hbm, vmem, vmem),
        scratch_shapes=[
            pltpu.VMEM((everything, sig + conv), half),
            pltpu.VMEM((everything, kv), half),
            pltpu.VMEM((kv_grad.shape[0], kv // 8), half),
            pltpu.VMEM((rows, kv // 8), half),
            dma((4,)),
            dma((groups,)),
            dma((groups,)),
            dma((2 * groups,)),
            dma((2 * groups,)),
            dma((2 * groups, 9)),
            dma((2 * groups, 9)),
            dma((2 * groups,)),
        ],
        compiler_params=pltpu.CompilerParams(
            collective_id=0, has_side_effects=True, vmem_limit_bytes=56 * 2**20
        ),
    )(sig_x, conv_x, sig_w, conv_w, kv_w, kv_grad, select)


def local_gathering(
    siglip_features,
    convnext_features,
    siglip_projection,
    convnext_projection,
    newline_embed,
    key_value_weight,
    tile_rank,
    row_end,
    key_value_grad,
    newline_grad,
):
    groups = lax.axis_size("dp")
    my_rank = lax.axis_index("dp")
    dest_rank, source, slot_place = tile_places(tile_rank, groups)
    per_device = dest_rank.shape[0] // groups
    capacity = 2 * per_device // groups
    row_count, sig = siglip_features.shape
    conv = convnext_features.shape[1]
    tile_rows = row_count // per_device
    kv = key_value_grad.shape[1]

    mine_dest = lax.dynamic_slice_in_dim(dest_rank, my_rank * per_device, per_device)
    mine_place = lax.dynamic_slice_in_dim(slot_place, my_rank * per_device, per_device)
    wanted = (mine_dest * capacity + mine_place)[:, None] * tile_rows + jnp.arange(
        tile_rows, dtype=jnp.int32
    )
    select = (
        wanted.reshape(row_count, 1)
        == jnp.arange(groups * capacity * tile_rows, dtype=jnp.int32)[None, :]
    ).astype(jnp.bfloat16)
    features, grads, projected, normed_grad = gather_and_project(
        siglip_features,
        convnext_features,
        siglip_projection,
        convnext_projection,
        key_value_weight,
        key_value_grad,
        select,
    )

    slot_global = source * capacity + slot_place
    line_live = (dest_rank == my_rank) & (row_end == 1)
    slot_ids = jnp.arange(groups * capacity, dtype=jnp.int32)[None, :]
    newline_mask = jnp.sum(
        ((slot_global[:, None] == slot_ids) & line_live[:, None]).astype(jnp.int32), axis=0
    )
    line_total = jnp.dot(
        newline_mask.astype(jnp.bfloat16)[None, :], newline_grad, preferred_element_type=jnp.float32
    )[0]
    line_total = lax.psum_scatter(line_total, "dp", scatter_dimension=0, tiled=True)
    line_vector = newline_embed.astype(jnp.float32)
    line_square = jnp.sum(line_vector * line_vector)

    proj_values = projected.astype(jnp.float32)
    grad_values = normed_grad.astype(jnp.float32)
    squares = jnp.sum(proj_values * proj_values, axis=1)
    products = jnp.sum(grad_values * proj_values, axis=1)
    squares, products, line_square = lax.psum((squares, products, line_square), ("section", "mp"))
    inverse = lax.rsqrt(squares / D + epsilon)[:, None]
    normed = (proj_values * inverse).astype(jnp.bfloat16)
    line_normed = (line_vector * lax.rsqrt(line_square / D + epsilon)).astype(jnp.bfloat16)
    projected_grad = (
        inverse * grad_values - inverse**3 * proj_values * products[:, None] / D
    ).astype(jnp.bfloat16)

    def block(x, first, width):
        return lax.dynamic_slice_in_dim(x, first + my_rank * (width // groups), width // groups, 1)

    def contract(a, b):
        return lax.dot_general(a, b, (((0,), (0,)), ((), ())), preferred_element_type=jnp.float32)

    siglip_result = contract(block(features, 0, sig), projected_grad)
    convnext_result = contract(block(features, sig, conv), projected_grad)
    kv_result = contract(block(grads, 0, kv), normed)
    kv_result = kv_result + line_total[:, None] * line_normed.astype(jnp.float32)[None, :]
    return (siglip_result, convnext_result, kv_result)


GATHER_LIMIT = 40 * 2**20


def local(*args):
    rows = lax.axis_size("dp") * args[0].shape[0]
    width = args[0].shape[1] + args[1].shape[1] + args[8].shape[1]
    plane = (lax.axis_size("section"), lax.axis_size("dp"), lax.axis_size("mp"))
    if 2 * rows * width <= GATHER_LIMIT and plane == (4, 4, 2):
        return local_gathering(*args)
    return local_reducing(*args)


def solution(mesh):
    in_specs = (
        P("dp", None),
        P("dp", None),
        P(None, ("section", "mp")),
        P(None, ("section", "mp")),
        P(("section", "mp")),
        P(None, ("section", "mp")),
        P(),
        P(),
        P("dp", None),
        P("dp", None),
    )
    out_specs = (P("dp", ("section", "mp")), P("dp", ("section", "mp")), P("dp", ("section", "mp")))
    return jax.shard_map(local, mesh=mesh, in_specs=in_specs, out_specs=out_specs, check_vma=False)
```

```python
import functools

import jax
import jax.numpy as jnp
from jax import lax
from jax.experimental import pallas as pl
from jax.experimental.pallas import tpu as pltpu
from jax.sharding import PartitionSpec as P

D = 8192


epsilon = 1e-06


def tile_places(tile_rank, groups):
    dest_rank = tile_rank[:, 0]
    tile_count = dest_rank.shape[0]
    per_device = tile_count // groups
    onehot = (dest_rank[:, None] == jnp.arange(groups, dtype=jnp.int32)[None, :]).astype(jnp.int32)
    blocks = onehot.reshape(groups, per_device, groups)
    before = jnp.cumsum(blocks, axis=1) - blocks
    slot_place = jnp.sum(before * blocks, axis=2).reshape(tile_count)
    source = jnp.arange(tile_count, dtype=jnp.int32) // per_device
    return (dest_rank, source, slot_place)


def row_norms(squares):
    return lax.psum((squares[0], squares[1]), ("section", "mp"))


def row_products(products):
    return lax.psum(products, ("section", "mp"))


def norm_backward(inverse_rms, grad_values, proj_values):
    products = row_products(jnp.sum(grad_values * proj_values, axis=1))[:, None]
    return (inverse_rms * grad_values - inverse_rms**3 * proj_values * products / D).astype(
        jnp.bfloat16
    )


def local_reducing(
    siglip_features,
    convnext_features,
    siglip_projection,
    convnext_projection,
    newline_embed,
    key_value_weight,
    tile_rank,
    row_end,
    key_value_grad,
    newline_grad,
):
    groups = lax.axis_size("dp")
    my_rank = lax.axis_index("dp")
    dest_rank, source, slot_place = tile_places(tile_rank, groups)
    per_device = dest_rank.shape[0] // groups
    capacity = 2 * per_device // groups
    row_count = siglip_features.shape[0]
    tile_rows = row_count // per_device
    share = siglip_projection.shape[1]
    mine_dest = lax.dynamic_slice_in_dim(dest_rank, my_rank * per_device, per_device)
    mine_place = lax.dynamic_slice_in_dim(slot_place, my_rank * per_device, per_device)
    rank_ids = jnp.arange(groups, dtype=jnp.int32)[:, None, None]
    place_ids = jnp.arange(capacity, dtype=jnp.int32)[None, :, None]
    select = (
        (mine_dest[None, None, :] == rank_ids) & (mine_place[None, None, :] == place_ids)
    ).astype(jnp.bfloat16)
    projected = (
        jnp.dot(siglip_features, siglip_projection, preferred_element_type=jnp.float32)
        + jnp.dot(convnext_features, convnext_projection, preferred_element_type=jnp.float32)
    ).astype(jnp.bfloat16)
    line_vector = newline_embed.astype(jnp.float32)
    line_square = jnp.sum(line_vector * line_vector)
    outgoing = jnp.einsum(
        "gcj,jtx->gctx",
        select,
        projected.reshape(per_device, tile_rows, share),
        preferred_element_type=jnp.float32,
    ).astype(jnp.bfloat16)
    outgoing = outgoing.reshape(groups, capacity * tile_rows, share)
    received = lax.all_to_all(outgoing, "dp", split_axis=0, concat_axis=0, tiled=True).reshape(
        groups * capacity * tile_rows, share
    )
    recv_values = received.astype(jnp.float32)
    statistic = row_norms((jnp.sum(recv_values * recv_values, axis=1), line_square))
    recv_inverse = lax.rsqrt(statistic[0] / D + epsilon)[:, None]
    line_total_sq = statistic[1]
    normed = (recv_values * recv_inverse).astype(jnp.bfloat16)
    line_normed = (line_vector * lax.rsqrt(line_total_sq / D + epsilon)).astype(jnp.bfloat16)
    slot_global = source * capacity + slot_place
    line_live = (dest_rank == my_rank) & (row_end == 1)
    slot_ids = jnp.arange(groups * capacity, dtype=jnp.int32)[None, :]
    newline_mask = jnp.sum(
        ((slot_global[:, None] == slot_ids) & line_live[:, None]).astype(jnp.int32), axis=0
    )
    line_total = jnp.dot(
        newline_mask.astype(jnp.bfloat16)[None, :], newline_grad, preferred_element_type=jnp.float32
    )[0]
    kv_term = lax.dot_general(
        key_value_grad, normed, (((0,), (0,)), ((), ())), preferred_element_type=jnp.float32
    )
    kv_term = kv_term + line_total[:, None] * line_normed.astype(jnp.float32)[None, :]
    normed_grad = jnp.dot(
        key_value_grad, key_value_weight, preferred_element_type=jnp.float32
    ).astype(jnp.bfloat16)
    returning = norm_backward(recv_inverse, normed_grad.astype(jnp.float32), recv_values)
    returned = lax.all_to_all(
        returning.reshape(groups, capacity * tile_rows, share),
        "dp",
        split_axis=0,
        concat_axis=0,
        tiled=True,
    )
    tile_back = jnp.einsum(
        "gcj,gctx->jtx",
        select,
        returned.reshape(groups, capacity, tile_rows, share),
        preferred_element_type=jnp.float32,
    ).reshape(row_count, share)
    projected_grad = tile_back.astype(jnp.bfloat16)
    contract = (((0,), (0,)), ((), ()))
    siglip_term = lax.dot_general(
        siglip_features, projected_grad, contract, preferred_element_type=jnp.float32
    )
    convnext_term = lax.dot_general(
        convnext_features, projected_grad, contract, preferred_element_type=jnp.float32
    )
    siglip_result, convnext_result, kv_result = (
        lax.psum_scatter(siglip_term, "dp", scatter_dimension=0, tiled=True),
        lax.psum_scatter(convnext_term, "dp", scatter_dimension=0, tiled=True),
        lax.psum_scatter(kv_term, "dp", scatter_dimension=0, tiled=True),
    )
    return (siglip_result, convnext_result, kv_result)


FROM_X, FROM_Y, FROM_CORE, HALF_X, HALF_Y, CORE_X, CORE_Y, CORE_HX, CORE_HY = range(9)
MESH = pl.DeviceIdType.MESH


def gather_kernel(
    groups,
    sig_ref,
    conv_ref,
    sig_w_ref,
    conv_w_ref,
    kv_w_ref,
    kv_grad,
    select,
    line_part,
    line_sq,
    f_out,
    g_out,
    p_out,
    n_out,
    stats_out,
    line_out,
    f,
    g,
    proj,
    ngrad,
    sig_w,
    conv_w,
    kv_w,
    acc,
    stats,
    line_all,
    slots,
    mine,
    local_sem,
    slot_send,
    slot_recv,
    line_send,
    line_recv,
    send,
    recv,
    out_sem,
    stat_send,
    stat_recv,
    sum_send,
    sum_recv,
):
    section = lax.axis_index("section")
    z = lax.axis_index("dp")
    y = lax.axis_index("mp")
    rows, sig = sig_ref.shape
    conv = conv_ref.shape[1]
    kv = kv_grad.shape[1]
    part = rows // 8
    wide = kv // 8
    slot_rows = kv_grad.shape[0] // groups
    x_section = lax.rem(section + 2, 4)
    core_section = section + 1 - 2 * lax.rem(section, 2)
    at_x = (x_section, z, y)
    at_y = (section, z, 1 - y)
    at_core = (core_section, z, y)

    def number(sec, yy):
        return sec * 2 + yy

    me = number(section, y)
    from_x, from_y = number(x_section, y), number(section, 1 - y)
    diag = number(x_section, 1 - y)
    core = [
        number(core_section, y),
        number(lax.rem(core_section + 2, 4), y),
        number(core_section, 1 - y),
        number(lax.rem(core_section + 2, 4), 1 - y),
    ]

    def peer(k):
        return (section, lax.rem(z + k, groups), y)

    def mate(j):
        p = lax.rem(me + j, 8)
        return (lax.div(p, 2), z, lax.rem(p, 2))

    weights = [
        pltpu.make_async_copy(sig_w_ref, sig_w, local_sem.at[4]),
        pltpu.make_async_copy(conv_w_ref, conv_w, local_sem.at[5]),
        pltpu.make_async_copy(kv_w_ref, kv_w, local_sem.at[6]),
    ]

    barrier = pltpu.get_barrier_semaphore()
    for device in [peer(k) for k in range(1, groups)] + [mate(j) for j in range(1, 8)]:
        pl.semaphore_signal(barrier, inc=1, device_id=device, device_id_type=MESH)
    pl.semaphore_wait(barrier, groups + 6)

    def shard(is_f, q, m, half=None):
        if is_f:
            first, count = q * rows + m * part, part
        else:
            first, count = q * rows, rows
        if half is not None:
            count //= 2
            first = first + half * count
        first = pl.multiple_of(first, 32)
        if is_f:
            return f.at[pl.ds(first, count), :]
        return g.at[pl.ds(first, count), pl.ds(pl.multiple_of(m * wide, 128), wide)]

    def remote(ref, device, ss, rs, dst=None):
        return pltpu.make_async_remote_copy(
            src_ref=ref,
            dst_ref=ref if dst is None else dst,
            send_sem=ss,
            recv_sem=rs,
            device_id=device,
            device_id_type=MESH,
        )

    sent = []
    own = pl.ds(pl.multiple_of(z * rows, rows), rows)
    my_cols = pl.ds(pl.multiple_of(me * wide, 128), wide)

    def slot_block(q):
        return pl.ds(pl.multiple_of(q * slot_rows, slot_rows), slot_rows)

    locals_ = [
        pltpu.make_async_copy(sig_ref, f.at[own, pl.ds(0, sig)], local_sem.at[0]),
        pltpu.make_async_copy(conv_ref, f.at[own, pl.ds(sig, conv)], local_sem.at[1]),
        pltpu.make_async_copy(
            kv_grad.at[slot_block(z), my_cols], slots.at[slot_block(z), :], local_sem.at[2]
        ),
    ]
    for copy in locals_:
        copy.start()
    for k in range(1, groups):
        copy = remote(
            kv_grad.at[slot_block(lax.rem(z + k, groups)), my_cols],
            peer(k),
            slot_send.at[k],
            slot_recv.at[k],
            slots.at[slot_block(z), :],
        )
        copy.start()
        sent.append(copy)
    for k in range(1, groups):
        copy = remote(
            line_part.at[lax.rem(z + k, groups)],
            peer(k),
            sum_send.at[k],
            sum_recv.at[k],
            line_all.at[z],
        )
        copy.start()
        sent.append(copy)
    line_all[z] = line_part[z]
    for copy in locals_:
        copy.wait()

    def line(is_f):
        for k in range(1, groups):
            at = (0 if is_f else groups) + k
            copy = remote(shard(is_f, z, me), peer(k), line_send.at[at], line_recv.at[at])
            copy.start()
            sent.append(copy)

    line(True)
    for copy in weights:
        copy.start()
    step = 256

    def compute(is_f, q):
        block = pl.ds(pl.multiple_of(q * rows, rows), rows)

        if not is_f:
            acc[...] = jnp.zeros_like(acc)

        @pl.loop(0, proj.shape[1] // step)
        def _(n):
            cols = pl.ds(pl.multiple_of(n * step, step), step)
            if is_f:
                total = jnp.dot(
                    f[block, :sig], sig_w[:, cols], preferred_element_type=jnp.float32
                ) + jnp.dot(f[block, sig:], conv_w[:, cols], preferred_element_type=jnp.float32)
                proj[block, cols] = total.astype(jnp.bfloat16)
            else:
                total = jnp.dot(g[block, :], kv_w[:, cols], preferred_element_type=jnp.float32)
                rounded = total.astype(jnp.bfloat16)
                ngrad[block, cols] = rounded
                gv = rounded.astype(jnp.float32)
                pv = proj[block, cols].astype(jnp.float32)
                sq, pr = pv * pv, gv * pv
                acc[0] += sq[:, :128] + sq[:, 128:]
                acc[1] += pr[:, :128] + pr[:, 128:]

    def share_stats(k):
        stats[me, k, 0:1, :] = jnp.sum(acc[0].T, axis=0, keepdims=True)
        stats[me, k, 1:2, :] = jnp.sum(acc[1].T, axis=0, keepdims=True)
        stats[me, k, 2:8, :] = line_sq[2:8, :]
        for j in range(1, 8):
            copy = remote(stats.at[me, k], mate(j), stat_send.at[k, j], stat_recv.at[k, j])
            copy.start()
            sent.append(copy)

    def result(is_f, k):
        q = lax.rem(z - k + groups, groups)
        block = pl.ds(pl.multiple_of(q * rows, rows), rows)
        here, there = (proj, p_out) if is_f else (ngrad, n_out)
        at = (2 if is_f else 3) * groups + k
        copy = pltpu.make_async_copy(here.at[block, :], there.at[block, :], out_sem.at[at])
        copy.start()
        written.append(copy)

    written = []

    def put(is_f, k):
        q = lax.rem(z - k + groups, groups)
        block = pl.ds(pl.multiple_of(q * rows, rows), rows)
        if is_f:
            copy = pltpu.make_async_copy(f.at[block, :], f_out.at[block, :], out_sem.at[k])
        else:
            copy = pltpu.make_async_copy(g.at[block, :], g_out.at[block, :], out_sem.at[groups + k])
        copy.start()
        written.append(copy)

    put(True, 0)
    for copy in weights:
        copy.wait()
    compute(True, z)
    result(True, 0)

    for k in range(1, groups):
        q = lax.rem(z - k + groups, groups)
        ref = slots.at[slot_block(q), :]
        remote(ref, peer(k), slot_send.at[k], slot_recv.at[k]).wait_recv()
    mine[...] = jnp.dot(select[...], slots[...], preferred_element_type=jnp.float32).astype(
        jnp.bfloat16
    )
    copy = pltpu.make_async_copy(mine, shard(False, z, me), local_sem.at[3])
    copy.start()
    copy.wait()
    line(False)

    items = [(False, 0), (True, 1), (True, 3), (True, 2), (False, 1), (False, 3), (False, 2)]

    def go(i, ref, device, kind):
        copy = remote(ref, device, send.at[i, kind], recv.at[i, kind])
        copy.start()
        sent.append(copy)

    def take(i, ref, kind):
        remote(ref, at_core, send.at[i, kind], recv.at[i, kind]).wait_recv()

    def owner(i):
        is_f, k = items[i]
        return is_f, lax.rem(z - k + groups, groups)

    def spread(i):
        is_f, q = owner(i)
        k = items[i][1]
        ref = shard(is_f, q, me)
        if k:
            at = (0 if is_f else groups) + k
            remote(ref, at_core, line_send.at[at], line_recv.at[at]).wait_recv()
        go(i, ref, at_x, FROM_X)
        go(i, ref, at_y, FROM_Y)
        go(i, ref, at_core, FROM_CORE)

    def forward(i):
        is_f, q = owner(i)
        take(i, shard(is_f, q, from_x), FROM_X)
        go(i, shard(is_f, q, from_x, 0), at_y, HALF_Y)
        go(i, shard(is_f, q, from_x), at_core, CORE_X)
        take(i, shard(is_f, q, from_y), FROM_Y)
        go(i, shard(is_f, q, from_y, 1), at_x, HALF_X)
        go(i, shard(is_f, q, from_y), at_core, CORE_Y)

    def halves(i):
        is_f, q = owner(i)
        take(i, shard(is_f, q, diag, 0), HALF_Y)
        go(i, shard(is_f, q, diag, 0), at_core, CORE_HY)
        take(i, shard(is_f, q, diag, 1), HALF_X)
        go(i, shard(is_f, q, diag, 1), at_core, CORE_HX)

    def finish(i):
        is_f, q = owner(i)
        take(i, shard(is_f, q, core[0]), FROM_CORE)
        take(i, shard(is_f, q, core[1]), CORE_X)
        take(i, shard(is_f, q, core[2]), CORE_Y)
        take(i, shard(is_f, q, core[3], 0), CORE_HY)
        take(i, shard(is_f, q, core[3], 1), CORE_HX)
        put(is_f, items[i][1])
        compute(is_f, q)
        if not is_f:
            share_stats(items[i][1])
        result(is_f, items[i][1])

    count = len(items)
    for t in range(count + 3):
        for lag, stage in enumerate((spread, forward, halves, finish)):
            if 0 <= t - lag < count:
                stage(t - lag)
    for k in range(1, groups):
        q = lax.rem(z - k + groups, groups)
        remote(line_all.at[q], peer(k), sum_send.at[k], sum_recv.at[k]).wait_recv()
    line_out[...] = sum([line_all[q] for q in range(1, groups)], line_all[0])
    for is_f, k in items:
        if is_f:
            continue
        for j in range(1, 8):
            ref = stats.at[lax.rem(me - j + 8, 8), k]
            remote(ref, mate(j), stat_send.at[k, j], stat_recv.at[k, j]).wait_recv()
        q = lax.rem(z - k + groups, groups)
        stats_out[:, pl.ds(pl.multiple_of(q * rows, rows), rows)] = sum(
            [stats[m, k] for m in range(1, 8)], stats[0, k]
        )
    for copy in sent:
        copy.wait_send()
    for copy in written:
        copy.wait()


def gather_and_project(sig_x, conv_x, sig_w, conv_w, kv_w, kv_grad, select, line_part, line_sq):
    groups = lax.axis_size("dp")
    rows, sig = sig_x.shape
    conv = conv_x.shape[1]
    kv = kv_grad.shape[1]
    share = sig_w.shape[1]
    everything = groups * rows
    half = jnp.bfloat16
    hbm = pl.BlockSpec(memory_space=pl.ANY)
    vmem = pl.BlockSpec(memory_space=pltpu.VMEM)
    dma = pltpu.SemaphoreType.DMA
    return pl.pallas_call(
        functools.partial(gather_kernel, groups),
        out_shape=(
            jax.ShapeDtypeStruct((everything, sig + conv), half),
            jax.ShapeDtypeStruct((everything, kv), half),
            jax.ShapeDtypeStruct((everything, share), half),
            jax.ShapeDtypeStruct((everything, share), half),
            jax.ShapeDtypeStruct((8, everything), jnp.float32),
            jax.ShapeDtypeStruct((8, kv // groups), jnp.float32),
        ),
        in_specs=[hbm, hbm, hbm, hbm, hbm, hbm, vmem, vmem, vmem],
        out_specs=(hbm, hbm, hbm, hbm, vmem, vmem),
        scratch_shapes=[
            pltpu.VMEM((everything, sig + conv), half),
            pltpu.VMEM((everything, kv), half),
            pltpu.VMEM((everything, share), half),
            pltpu.VMEM((everything, share), half),
            pltpu.VMEM(sig_w.shape, half),
            pltpu.VMEM(conv_w.shape, half),
            pltpu.VMEM(kv_w.shape, half),
            pltpu.VMEM((2, rows, 128), jnp.float32),
            pltpu.VMEM((8, groups, 8, rows), jnp.float32),
            pltpu.VMEM((groups, 8, kv // groups), jnp.float32),
            pltpu.VMEM((kv_grad.shape[0], kv // 8), half),
            pltpu.VMEM((rows, kv // 8), half),
            dma((7,)),
            dma((groups,)),
            dma((groups,)),
            dma((2 * groups,)),
            dma((2 * groups,)),
            dma((2 * groups, 9)),
            dma((2 * groups, 9)),
            dma((4 * groups,)),
            dma((groups, 8)),
            dma((groups, 8)),
            dma((groups,)),
            dma((groups,)),
        ],
        compiler_params=pltpu.CompilerParams(
            collective_id=0, has_side_effects=True, vmem_limit_bytes=56 * 2**20
        ),
    )(sig_x, conv_x, sig_w, conv_w, kv_w, kv_grad, select, line_part, line_sq)


def local_gathering(
    siglip_features,
    convnext_features,
    siglip_projection,
    convnext_projection,
    newline_embed,
    key_value_weight,
    tile_rank,
    row_end,
    key_value_grad,
    newline_grad,
):
    groups = lax.axis_size("dp")
    my_rank = lax.axis_index("dp")
    dest_rank, source, slot_place = tile_places(tile_rank, groups)
    per_device = dest_rank.shape[0] // groups
    capacity = 2 * per_device // groups
    row_count, sig = siglip_features.shape
    conv = convnext_features.shape[1]
    tile_rows = row_count // per_device
    kv = key_value_grad.shape[1]

    mine_dest = lax.dynamic_slice_in_dim(dest_rank, my_rank * per_device, per_device)
    mine_place = lax.dynamic_slice_in_dim(slot_place, my_rank * per_device, per_device)
    wanted = (mine_dest * capacity + mine_place)[:, None] * tile_rows + jnp.arange(
        tile_rows, dtype=jnp.int32
    )
    select = (
        wanted.reshape(row_count, 1)
        == jnp.arange(groups * capacity * tile_rows, dtype=jnp.int32)[None, :]
    ).astype(jnp.bfloat16)
    slot_global = source * capacity + slot_place
    line_live = (dest_rank == my_rank) & (row_end == 1)
    slot_ids = jnp.arange(groups * capacity, dtype=jnp.int32)[None, :]
    newline_mask = jnp.sum(
        ((slot_global[:, None] == slot_ids) & line_live[:, None]).astype(jnp.int32), axis=0
    )
    line_total = jnp.dot(
        newline_mask.astype(jnp.bfloat16)[None, :], newline_grad, preferred_element_type=jnp.float32
    )[0]
    line_part = jnp.broadcast_to(
        line_total.reshape(groups, 1, kv // groups), (groups, 8, kv // groups)
    )
    line_vector = newline_embed.astype(jnp.float32)
    line_square = jnp.sum(line_vector * line_vector)
    features, grads, projected, normed_grad, stats, line_total = gather_and_project(
        siglip_features,
        convnext_features,
        siglip_projection,
        convnext_projection,
        key_value_weight,
        key_value_grad,
        select,
        line_part,
        jnp.full((8, row_count), line_square),
    )
    squares, products, line_square = stats[0], stats[1], stats[2, 0]
    line_total = line_total[0]

    proj_values = projected.astype(jnp.float32)
    grad_values = normed_grad.astype(jnp.float32)
    inverse = lax.rsqrt(squares / D + epsilon)[:, None]
    normed = (proj_values * inverse).astype(jnp.bfloat16)
    line_normed = (line_vector * lax.rsqrt(line_square / D + epsilon)).astype(jnp.bfloat16)
    projected_grad = (
        inverse * grad_values - inverse**3 * proj_values * products[:, None] / D
    ).astype(jnp.bfloat16)

    def block(x, first, width):
        return lax.dynamic_slice_in_dim(x, first + my_rank * (width // groups), width // groups, 1)

    def contract(a, b):
        return lax.dot_general(a, b, (((0,), (0,)), ((), ())), preferred_element_type=jnp.float32)

    siglip_result = contract(block(features, 0, sig), projected_grad)
    convnext_result = contract(block(features, sig, conv), projected_grad)
    kv_result = contract(block(grads, 0, kv), normed)
    kv_result = kv_result + line_total[:, None] * line_normed.astype(jnp.float32)[None, :]
    return (siglip_result, convnext_result, kv_result)


GATHER_LIMIT = 40 * 2**20


def local(*args):
    rows = lax.axis_size("dp") * args[0].shape[0]
    width = args[0].shape[1] + args[1].shape[1] + args[8].shape[1]
    plane = (lax.axis_size("section"), lax.axis_size("dp"), lax.axis_size("mp"))
    if 2 * rows * width <= GATHER_LIMIT and plane == (4, 4, 2):
        return local_gathering(*args)
    return local_reducing(*args)


def solution(mesh):
    in_specs = (
        P("dp", None),
        P("dp", None),
        P(None, ("section", "mp")),
        P(None, ("section", "mp")),
        P(("section", "mp")),
        P(None, ("section", "mp")),
        P(),
        P(),
        P("dp", None),
        P("dp", None),
    )
    out_specs = (P("dp", ("section", "mp")), P("dp", ("section", "mp")), P("dp", ("section", "mp")))
    return jax.shard_map(local, mesh=mesh, in_specs=in_specs, out_specs=out_specs, check_vma=False)
```

```python
import functools

import jax
import jax.numpy as jnp
from jax import lax
from jax.experimental import pallas as pl
from jax.experimental.pallas import tpu as pltpu
from jax.sharding import PartitionSpec as P

D = 8192


epsilon = 1e-06


def tile_places(tile_rank, groups):
    dest_rank = tile_rank[:, 0]
    tile_count = dest_rank.shape[0]
    per_device = tile_count // groups
    onehot = (dest_rank[:, None] == jnp.arange(groups, dtype=jnp.int32)[None, :]).astype(jnp.int32)
    blocks = onehot.reshape(groups, per_device, groups)
    before = jnp.cumsum(blocks, axis=1) - blocks
    slot_place = jnp.sum(before * blocks, axis=2).reshape(tile_count)
    source = jnp.arange(tile_count, dtype=jnp.int32) // per_device
    return (dest_rank, source, slot_place)


def row_norms(squares):
    return lax.psum((squares[0], squares[1]), ("section", "mp"))


def row_products(products):
    return lax.psum(products, ("section", "mp"))


def norm_backward(inverse_rms, grad_values, proj_values):
    products = row_products(jnp.sum(grad_values * proj_values, axis=1))[:, None]
    return (inverse_rms * grad_values - inverse_rms**3 * proj_values * products / D).astype(
        jnp.bfloat16
    )


def local_reducing(
    siglip_features,
    convnext_features,
    siglip_projection,
    convnext_projection,
    newline_embed,
    key_value_weight,
    tile_rank,
    row_end,
    key_value_grad,
    newline_grad,
):
    groups = lax.axis_size("dp")
    my_rank = lax.axis_index("dp")
    dest_rank, source, slot_place = tile_places(tile_rank, groups)
    per_device = dest_rank.shape[0] // groups
    capacity = 2 * per_device // groups
    row_count = siglip_features.shape[0]
    tile_rows = row_count // per_device
    share = siglip_projection.shape[1]
    mine_dest = lax.dynamic_slice_in_dim(dest_rank, my_rank * per_device, per_device)
    mine_place = lax.dynamic_slice_in_dim(slot_place, my_rank * per_device, per_device)
    rank_ids = jnp.arange(groups, dtype=jnp.int32)[:, None, None]
    place_ids = jnp.arange(capacity, dtype=jnp.int32)[None, :, None]
    select = (
        (mine_dest[None, None, :] == rank_ids) & (mine_place[None, None, :] == place_ids)
    ).astype(jnp.bfloat16)
    projected = (
        jnp.dot(siglip_features, siglip_projection, preferred_element_type=jnp.float32)
        + jnp.dot(convnext_features, convnext_projection, preferred_element_type=jnp.float32)
    ).astype(jnp.bfloat16)
    line_vector = newline_embed.astype(jnp.float32)
    line_square = jnp.sum(line_vector * line_vector)
    outgoing = jnp.einsum(
        "gcj,jtx->gctx",
        select,
        projected.reshape(per_device, tile_rows, share),
        preferred_element_type=jnp.float32,
    ).astype(jnp.bfloat16)
    outgoing = outgoing.reshape(groups, capacity * tile_rows, share)
    received = lax.all_to_all(outgoing, "dp", split_axis=0, concat_axis=0, tiled=True).reshape(
        groups * capacity * tile_rows, share
    )
    recv_values = received.astype(jnp.float32)
    statistic = row_norms((jnp.sum(recv_values * recv_values, axis=1), line_square))
    recv_inverse = lax.rsqrt(statistic[0] / D + epsilon)[:, None]
    line_total_sq = statistic[1]
    normed = (recv_values * recv_inverse).astype(jnp.bfloat16)
    line_normed = (line_vector * lax.rsqrt(line_total_sq / D + epsilon)).astype(jnp.bfloat16)
    slot_global = source * capacity + slot_place
    line_live = (dest_rank == my_rank) & (row_end == 1)
    slot_ids = jnp.arange(groups * capacity, dtype=jnp.int32)[None, :]
    newline_mask = jnp.sum(
        ((slot_global[:, None] == slot_ids) & line_live[:, None]).astype(jnp.int32), axis=0
    )
    line_total = jnp.dot(
        newline_mask.astype(jnp.bfloat16)[None, :], newline_grad, preferred_element_type=jnp.float32
    )[0]
    kv_term = lax.dot_general(
        key_value_grad, normed, (((0,), (0,)), ((), ())), preferred_element_type=jnp.float32
    )
    kv_term = kv_term + line_total[:, None] * line_normed.astype(jnp.float32)[None, :]
    normed_grad = jnp.dot(
        key_value_grad, key_value_weight, preferred_element_type=jnp.float32
    ).astype(jnp.bfloat16)
    returning = norm_backward(recv_inverse, normed_grad.astype(jnp.float32), recv_values)
    returned = lax.all_to_all(
        returning.reshape(groups, capacity * tile_rows, share),
        "dp",
        split_axis=0,
        concat_axis=0,
        tiled=True,
    )
    tile_back = jnp.einsum(
        "gcj,gctx->jtx",
        select,
        returned.reshape(groups, capacity, tile_rows, share),
        preferred_element_type=jnp.float32,
    ).reshape(row_count, share)
    projected_grad = tile_back.astype(jnp.bfloat16)
    contract = (((0,), (0,)), ((), ()))
    siglip_term = lax.dot_general(
        siglip_features, projected_grad, contract, preferred_element_type=jnp.float32
    )
    convnext_term = lax.dot_general(
        convnext_features, projected_grad, contract, preferred_element_type=jnp.float32
    )
    siglip_result, convnext_result, kv_result = (
        lax.psum_scatter(siglip_term, "dp", scatter_dimension=0, tiled=True),
        lax.psum_scatter(convnext_term, "dp", scatter_dimension=0, tiled=True),
        lax.psum_scatter(kv_term, "dp", scatter_dimension=0, tiled=True),
    )
    return (siglip_result, convnext_result, kv_result)


FROM_X, FROM_Y, FROM_CORE, HALF_X, HALF_Y, CORE_X, CORE_Y, CORE_HX, CORE_HY = range(9)
MESH = pl.DeviceIdType.MESH


def gather_kernel(
    groups,
    sig_ref,
    conv_ref,
    sig_w_ref,
    conv_w_ref,
    kv_w_ref,
    kv_grad,
    select,
    line_part,
    line_sq,
    f_out,
    g_out,
    p_out,
    n_out,
    stats_out,
    line_out,
    f,
    g,
    proj,
    ngrad,
    sig_w,
    conv_w,
    kv_w,
    acc,
    stats,
    line_all,
    slots,
    mine,
    local_sem,
    slot_send,
    slot_recv,
    line_send,
    line_recv,
    send,
    recv,
    out_sem,
    stat_send,
    stat_recv,
    sum_send,
    sum_recv,
):
    section = lax.axis_index("section")
    z = lax.axis_index("dp")
    y = lax.axis_index("mp")
    rows, sig = sig_ref.shape
    conv = conv_ref.shape[1]
    kv = kv_grad.shape[1]
    part = rows // 8
    wide = kv // 8
    slot_rows = kv_grad.shape[0] // groups
    x_section = lax.rem(section + 2, 4)
    core_section = section + 1 - 2 * lax.rem(section, 2)
    at_x = (x_section, z, y)
    at_y = (section, z, 1 - y)
    at_core = (core_section, z, y)

    def number(sec, yy):
        return sec * 2 + yy

    me = number(section, y)
    from_x, from_y = number(x_section, y), number(section, 1 - y)
    diag = number(x_section, 1 - y)
    core = [
        number(core_section, y),
        number(lax.rem(core_section + 2, 4), y),
        number(core_section, 1 - y),
        number(lax.rem(core_section + 2, 4), 1 - y),
    ]

    def peer(k):
        return (section, lax.rem(z + k, groups), y)

    def mate(j):
        p = lax.rem(me + j, 8)
        return (lax.div(p, 2), z, lax.rem(p, 2))

    weights = [
        pltpu.make_async_copy(sig_w_ref, sig_w, local_sem.at[4]),
        pltpu.make_async_copy(conv_w_ref, conv_w, local_sem.at[5]),
        pltpu.make_async_copy(kv_w_ref, kv_w, local_sem.at[6]),
    ]

    barrier = pltpu.get_barrier_semaphore()
    for device in [peer(k) for k in range(1, groups)] + [mate(j) for j in range(1, 8)]:
        pl.semaphore_signal(barrier, inc=1, device_id=device, device_id_type=MESH)
    pl.semaphore_wait(barrier, groups + 6)

    def shard(is_f, q, m, half=None):
        if is_f:
            first, count = q * rows + m * part, part
        else:
            first, count = q * rows, rows
        if half is not None:
            count //= 2
            first = first + half * count
        first = pl.multiple_of(first, 32)
        if is_f:
            return f.at[pl.ds(first, count), :]
        return g.at[pl.ds(first, count), pl.ds(pl.multiple_of(m * wide, 128), wide)]

    def remote(ref, device, ss, rs, dst=None):
        return pltpu.make_async_remote_copy(
            src_ref=ref,
            dst_ref=ref if dst is None else dst,
            send_sem=ss,
            recv_sem=rs,
            device_id=device,
            device_id_type=MESH,
        )

    sent = []
    own = pl.ds(pl.multiple_of(z * rows, rows), rows)
    my_cols = pl.ds(pl.multiple_of(me * wide, 128), wide)

    def slot_block(q):
        return pl.ds(pl.multiple_of(q * slot_rows, slot_rows), slot_rows)

    locals_ = [
        pltpu.make_async_copy(sig_ref, f.at[own, pl.ds(0, sig)], local_sem.at[0]),
        pltpu.make_async_copy(conv_ref, f.at[own, pl.ds(sig, conv)], local_sem.at[1]),
        pltpu.make_async_copy(
            kv_grad.at[slot_block(z), my_cols], slots.at[slot_block(z), :], local_sem.at[2]
        ),
    ]
    for copy in locals_:
        copy.start()
    for k in range(1, groups):
        copy = remote(
            kv_grad.at[slot_block(lax.rem(z + k, groups)), my_cols],
            peer(k),
            slot_send.at[k],
            slot_recv.at[k],
            slots.at[slot_block(z), :],
        )
        copy.start()
        sent.append(copy)
    for k in range(1, groups):
        copy = remote(
            line_part.at[lax.rem(z + k, groups)],
            peer(k),
            sum_send.at[k],
            sum_recv.at[k],
            line_all.at[z],
        )
        copy.start()
        sent.append(copy)
    line_all[z] = line_part[z]
    for copy in locals_:
        copy.wait()

    def line(is_f):
        for k in (1, 3, 2):
            at = (0 if is_f else groups) + k
            copy = remote(shard(is_f, z, me), peer(k), line_send.at[at], line_recv.at[at])
            copy.start()
            sent.append(copy)

    line(True)
    for copy in weights:
        copy.start()
    step = 256

    def compute(is_f, q):
        block = pl.ds(pl.multiple_of(q * rows, rows), rows)

        if not is_f:
            acc[...] = jnp.zeros_like(acc)

        @pl.loop(0, proj.shape[1] // step)
        def _(n):
            cols = pl.ds(pl.multiple_of(n * step, step), step)
            if is_f:
                total = jnp.dot(
                    f[block, :sig], sig_w[:, cols], preferred_element_type=jnp.float32
                ) + jnp.dot(f[block, sig:], conv_w[:, cols], preferred_element_type=jnp.float32)
                proj[block, cols] = total.astype(jnp.bfloat16)
            else:
                total = jnp.dot(g[block, :], kv_w[:, cols], preferred_element_type=jnp.float32)
                rounded = total.astype(jnp.bfloat16)
                ngrad[block, cols] = rounded
                gv = rounded.astype(jnp.float32)
                pv = proj[block, cols].astype(jnp.float32)
                sq, pr = pv * pv, gv * pv
                acc[0] += sq[:, :128] + sq[:, 128:]
                acc[1] += pr[:, :128] + pr[:, 128:]

    def share_stats(k):
        stats[me, k, 0:1, :] = jnp.sum(acc[0].T, axis=0, keepdims=True)
        stats[me, k, 1:2, :] = jnp.sum(acc[1].T, axis=0, keepdims=True)
        stats[me, k, 2:8, :] = line_sq[2:8, :]
        for j in range(1, 8):
            copy = remote(stats.at[me, k], mate(j), stat_send.at[k, j], stat_recv.at[k, j])
            copy.start()
            sent.append(copy)

    def result(is_f, k):
        q = lax.rem(z - k + groups, groups)
        block = pl.ds(pl.multiple_of(q * rows, rows), rows)
        here, there = (proj, p_out) if is_f else (ngrad, n_out)
        at = (2 if is_f else 3) * groups + k
        copy = pltpu.make_async_copy(here.at[block, :], there.at[block, :], out_sem.at[at])
        copy.start()
        written.append(copy)

    written = []

    def put(is_f, k):
        q = lax.rem(z - k + groups, groups)
        block = pl.ds(pl.multiple_of(q * rows, rows), rows)
        if is_f:
            copy = pltpu.make_async_copy(f.at[block, :], f_out.at[block, :], out_sem.at[k])
        else:
            copy = pltpu.make_async_copy(g.at[block, :], g_out.at[block, :], out_sem.at[groups + k])
        copy.start()
        written.append(copy)

    put(True, 0)
    for copy in weights:
        copy.wait()
    compute(True, z)
    result(True, 0)

    for k in range(1, groups):
        q = lax.rem(z - k + groups, groups)
        ref = slots.at[slot_block(q), :]
        remote(ref, peer(k), slot_send.at[k], slot_recv.at[k]).wait_recv()
    mine[...] = jnp.dot(select[...], slots[...], preferred_element_type=jnp.float32).astype(
        jnp.bfloat16
    )
    copy = pltpu.make_async_copy(mine, shard(False, z, me), local_sem.at[3])
    copy.start()
    copy.wait()
    line(False)

    items = [(False, 0), (True, 1), (True, 3), (True, 2), (False, 1), (False, 3), (False, 2)]

    def go(i, ref, device, kind):
        copy = remote(ref, device, send.at[i, kind], recv.at[i, kind])
        copy.start()
        sent.append(copy)

    def take(i, ref, kind):
        remote(ref, at_core, send.at[i, kind], recv.at[i, kind]).wait_recv()

    def owner(i):
        is_f, k = items[i]
        return is_f, lax.rem(z - k + groups, groups)

    def spread(i):
        is_f, q = owner(i)
        k = items[i][1]
        ref = shard(is_f, q, me)
        if k:
            at = (0 if is_f else groups) + k
            remote(ref, at_core, line_send.at[at], line_recv.at[at]).wait_recv()
        go(i, ref, at_x, FROM_X)
        go(i, ref, at_y, FROM_Y)
        go(i, ref, at_core, FROM_CORE)

    def forward(i):
        is_f, q = owner(i)
        take(i, shard(is_f, q, from_x), FROM_X)
        go(i, shard(is_f, q, from_x, 0), at_y, HALF_Y)
        go(i, shard(is_f, q, from_x), at_core, CORE_X)
        take(i, shard(is_f, q, from_y), FROM_Y)
        go(i, shard(is_f, q, from_y, 1), at_x, HALF_X)
        go(i, shard(is_f, q, from_y), at_core, CORE_Y)

    def halves(i):
        is_f, q = owner(i)
        take(i, shard(is_f, q, diag, 0), HALF_Y)
        go(i, shard(is_f, q, diag, 0), at_core, CORE_HY)
        take(i, shard(is_f, q, diag, 1), HALF_X)
        go(i, shard(is_f, q, diag, 1), at_core, CORE_HX)

    def finish(i):
        is_f, q = owner(i)
        take(i, shard(is_f, q, core[0]), FROM_CORE)
        take(i, shard(is_f, q, core[1]), CORE_X)
        take(i, shard(is_f, q, core[2]), CORE_Y)
        take(i, shard(is_f, q, core[3], 0), CORE_HY)
        take(i, shard(is_f, q, core[3], 1), CORE_HX)
        put(is_f, items[i][1])
        compute(is_f, q)
        if not is_f:
            share_stats(items[i][1])
        result(is_f, items[i][1])

    order = [
        (spread, 0), (spread, 1), (forward, 0), (spread, 2), (forward, 1), (halves, 0),
        (spread, 3), (forward, 2), (halves, 1), (finish, 0), (forward, 3), (halves, 2),
        (spread, 4), (finish, 1), (halves, 3), (spread, 5), (finish, 2), (forward, 4),
        (halves, 4), (spread, 6), (finish, 3), (forward, 5), (halves, 5), (forward, 6),
        (finish, 4), (halves, 6), (finish, 5), (finish, 6),
    ]
    for stage, i in order:
        stage(i)
    for k in range(1, groups):
        q = lax.rem(z - k + groups, groups)
        remote(line_all.at[q], peer(k), sum_send.at[k], sum_recv.at[k]).wait_recv()
    line_out[...] = sum([line_all[q] for q in range(1, groups)], line_all[0])
    for is_f, k in items:
        if is_f:
            continue
        for j in range(1, 8):
            ref = stats.at[lax.rem(me - j + 8, 8), k]
            remote(ref, mate(j), stat_send.at[k, j], stat_recv.at[k, j]).wait_recv()
        q = lax.rem(z - k + groups, groups)
        stats_out[:, pl.ds(pl.multiple_of(q * rows, rows), rows)] = sum(
            [stats[m, k] for m in range(1, 8)], stats[0, k]
        )
    for copy in sent:
        copy.wait_send()
    for copy in written:
        copy.wait()


def gather_and_project(sig_x, conv_x, sig_w, conv_w, kv_w, kv_grad, select, line_part, line_sq):
    groups = lax.axis_size("dp")
    rows, sig = sig_x.shape
    conv = conv_x.shape[1]
    kv = kv_grad.shape[1]
    share = sig_w.shape[1]
    everything = groups * rows
    half = jnp.bfloat16
    hbm = pl.BlockSpec(memory_space=pl.ANY)
    vmem = pl.BlockSpec(memory_space=pltpu.VMEM)
    dma = pltpu.SemaphoreType.DMA
    return pl.pallas_call(
        functools.partial(gather_kernel, groups),
        out_shape=(
            jax.ShapeDtypeStruct((everything, sig + conv), half),
            jax.ShapeDtypeStruct((everything, kv), half),
            jax.ShapeDtypeStruct((everything, share), half),
            jax.ShapeDtypeStruct((everything, share), half),
            jax.ShapeDtypeStruct((8, everything), jnp.float32),
            jax.ShapeDtypeStruct((8, kv // groups), jnp.float32),
        ),
        in_specs=[hbm, hbm, hbm, hbm, hbm, hbm, vmem, vmem, vmem],
        out_specs=(hbm, hbm, hbm, hbm, vmem, vmem),
        scratch_shapes=[
            pltpu.VMEM((everything, sig + conv), half),
            pltpu.VMEM((everything, kv), half),
            pltpu.VMEM((everything, share), half),
            pltpu.VMEM((everything, share), half),
            pltpu.VMEM(sig_w.shape, half),
            pltpu.VMEM(conv_w.shape, half),
            pltpu.VMEM(kv_w.shape, half),
            pltpu.VMEM((2, rows, 128), jnp.float32),
            pltpu.VMEM((8, groups, 8, rows), jnp.float32),
            pltpu.VMEM((groups, 8, kv // groups), jnp.float32),
            pltpu.VMEM((kv_grad.shape[0], kv // 8), half),
            pltpu.VMEM((rows, kv // 8), half),
            dma((7,)),
            dma((groups,)),
            dma((groups,)),
            dma((2 * groups,)),
            dma((2 * groups,)),
            dma((2 * groups, 9)),
            dma((2 * groups, 9)),
            dma((4 * groups,)),
            dma((groups, 8)),
            dma((groups, 8)),
            dma((groups,)),
            dma((groups,)),
        ],
        compiler_params=pltpu.CompilerParams(
            collective_id=0, has_side_effects=True, vmem_limit_bytes=56 * 2**20
        ),
    )(sig_x, conv_x, sig_w, conv_w, kv_w, kv_grad, select, line_part, line_sq)


def local_gathering(
    siglip_features,
    convnext_features,
    siglip_projection,
    convnext_projection,
    newline_embed,
    key_value_weight,
    tile_rank,
    row_end,
    key_value_grad,
    newline_grad,
):
    groups = lax.axis_size("dp")
    my_rank = lax.axis_index("dp")
    dest_rank, source, slot_place = tile_places(tile_rank, groups)
    per_device = dest_rank.shape[0] // groups
    capacity = 2 * per_device // groups
    row_count, sig = siglip_features.shape
    conv = convnext_features.shape[1]
    tile_rows = row_count // per_device
    kv = key_value_grad.shape[1]

    mine_dest = lax.dynamic_slice_in_dim(dest_rank, my_rank * per_device, per_device)
    mine_place = lax.dynamic_slice_in_dim(slot_place, my_rank * per_device, per_device)
    wanted = (mine_dest * capacity + mine_place)[:, None] * tile_rows + jnp.arange(
        tile_rows, dtype=jnp.int32
    )
    select = (
        wanted.reshape(row_count, 1)
        == jnp.arange(groups * capacity * tile_rows, dtype=jnp.int32)[None, :]
    ).astype(jnp.bfloat16)
    slot_global = source * capacity + slot_place
    line_live = (dest_rank == my_rank) & (row_end == 1)
    slot_ids = jnp.arange(groups * capacity, dtype=jnp.int32)[None, :]
    newline_mask = jnp.sum(
        ((slot_global[:, None] == slot_ids) & line_live[:, None]).astype(jnp.int32), axis=0
    )
    line_total = jnp.dot(
        newline_mask.astype(jnp.bfloat16)[None, :], newline_grad, preferred_element_type=jnp.float32
    )[0]
    line_part = jnp.broadcast_to(
        line_total.reshape(groups, 1, kv // groups), (groups, 8, kv // groups)
    )
    line_vector = newline_embed.astype(jnp.float32)
    line_square = jnp.sum(line_vector * line_vector)
    features, grads, projected, normed_grad, stats, line_total = gather_and_project(
        siglip_features,
        convnext_features,
        siglip_projection,
        convnext_projection,
        key_value_weight,
        key_value_grad,
        select,
        line_part,
        jnp.full((8, row_count), line_square),
    )
    squares, products, line_square = stats[0], stats[1], stats[2, 0]
    line_total = line_total[0]

    proj_values = projected.astype(jnp.float32)
    grad_values = normed_grad.astype(jnp.float32)
    inverse = lax.rsqrt(squares / D + epsilon)[:, None]
    normed = (proj_values * inverse).astype(jnp.bfloat16)
    line_normed = (line_vector * lax.rsqrt(line_square / D + epsilon)).astype(jnp.bfloat16)
    projected_grad = (
        inverse * grad_values - inverse**3 * proj_values * products[:, None] / D
    ).astype(jnp.bfloat16)

    def block(x, first, width):
        return lax.dynamic_slice_in_dim(x, first + my_rank * (width // groups), width // groups, 1)

    def contract(a, b):
        return lax.dot_general(a, b, (((0,), (0,)), ((), ())), preferred_element_type=jnp.float32)

    siglip_result = contract(block(features, 0, sig), projected_grad)
    convnext_result = contract(block(features, sig, conv), projected_grad)
    kv_result = contract(block(grads, 0, kv), normed)
    kv_result = kv_result + line_total[:, None] * line_normed.astype(jnp.float32)[None, :]
    return (siglip_result, convnext_result, kv_result)


GATHER_LIMIT = 40 * 2**20


def local(*args):
    rows = lax.axis_size("dp") * args[0].shape[0]
    width = args[0].shape[1] + args[1].shape[1] + args[8].shape[1]
    plane = (lax.axis_size("section"), lax.axis_size("dp"), lax.axis_size("mp"))
    if 2 * rows * width <= GATHER_LIMIT and plane == (4, 4, 2):
        return local_gathering(*args)
    return local_reducing(*args)


def solution(mesh):
    in_specs = (
        P("dp", None),
        P("dp", None),
        P(None, ("section", "mp")),
        P(None, ("section", "mp")),
        P(("section", "mp")),
        P(None, ("section", "mp")),
        P(),
        P(),
        P("dp", None),
        P("dp", None),
    )
    out_specs = (P("dp", ("section", "mp")), P("dp", ("section", "mp")), P("dp", ("section", "mp")))
    return jax.shard_map(local, mesh=mesh, in_specs=in_specs, out_specs=out_specs, check_vma=False)
```

```python
import functools

import jax
import jax.numpy as jnp
from jax import lax
from jax.experimental import pallas as pl
from jax.experimental.pallas import tpu as pltpu
from jax.sharding import PartitionSpec as P

D = 8192


epsilon = 1e-06


def tile_places(tile_rank, groups):
    dest_rank = tile_rank[:, 0]
    tile_count = dest_rank.shape[0]
    per_device = tile_count // groups
    onehot = (dest_rank[:, None] == jnp.arange(groups, dtype=jnp.int32)[None, :]).astype(jnp.int32)
    blocks = onehot.reshape(groups, per_device, groups)
    before = jnp.cumsum(blocks, axis=1) - blocks
    slot_place = jnp.sum(before * blocks, axis=2).reshape(tile_count)
    source = jnp.arange(tile_count, dtype=jnp.int32) // per_device
    return (dest_rank, source, slot_place)


def row_norms(squares):
    return lax.psum((squares[0], squares[1]), ("section", "mp"))


def row_products(products):
    return lax.psum(products, ("section", "mp"))


def norm_backward(inverse_rms, grad_values, proj_values):
    products = row_products(jnp.sum(grad_values * proj_values, axis=1))[:, None]
    return (inverse_rms * grad_values - inverse_rms**3 * proj_values * products / D).astype(
        jnp.bfloat16
    )


def local_reducing(
    siglip_features,
    convnext_features,
    siglip_projection,
    convnext_projection,
    newline_embed,
    key_value_weight,
    tile_rank,
    row_end,
    key_value_grad,
    newline_grad,
):
    groups = lax.axis_size("dp")
    my_rank = lax.axis_index("dp")
    dest_rank, source, slot_place = tile_places(tile_rank, groups)
    per_device = dest_rank.shape[0] // groups
    capacity = 2 * per_device // groups
    row_count = siglip_features.shape[0]
    tile_rows = row_count // per_device
    share = siglip_projection.shape[1]
    mine_dest = lax.dynamic_slice_in_dim(dest_rank, my_rank * per_device, per_device)
    mine_place = lax.dynamic_slice_in_dim(slot_place, my_rank * per_device, per_device)
    rank_ids = jnp.arange(groups, dtype=jnp.int32)[:, None, None]
    place_ids = jnp.arange(capacity, dtype=jnp.int32)[None, :, None]
    select = (
        (mine_dest[None, None, :] == rank_ids) & (mine_place[None, None, :] == place_ids)
    ).astype(jnp.bfloat16)
    projected = (
        jnp.dot(siglip_features, siglip_projection, preferred_element_type=jnp.float32)
        + jnp.dot(convnext_features, convnext_projection, preferred_element_type=jnp.float32)
    ).astype(jnp.bfloat16)
    line_vector = newline_embed.astype(jnp.float32)
    line_square = jnp.sum(line_vector * line_vector)
    outgoing = jnp.einsum(
        "gcj,jtx->gctx",
        select,
        projected.reshape(per_device, tile_rows, share),
        preferred_element_type=jnp.float32,
    ).astype(jnp.bfloat16)
    outgoing = outgoing.reshape(groups, capacity * tile_rows, share)
    received = lax.all_to_all(outgoing, "dp", split_axis=0, concat_axis=0, tiled=True).reshape(
        groups * capacity * tile_rows, share
    )
    recv_values = received.astype(jnp.float32)
    statistic = row_norms((jnp.sum(recv_values * recv_values, axis=1), line_square))
    recv_inverse = lax.rsqrt(statistic[0] / D + epsilon)[:, None]
    line_total_sq = statistic[1]
    normed = (recv_values * recv_inverse).astype(jnp.bfloat16)
    line_normed = (line_vector * lax.rsqrt(line_total_sq / D + epsilon)).astype(jnp.bfloat16)
    slot_global = source * capacity + slot_place
    line_live = (dest_rank == my_rank) & (row_end == 1)
    slot_ids = jnp.arange(groups * capacity, dtype=jnp.int32)[None, :]
    newline_mask = jnp.sum(
        ((slot_global[:, None] == slot_ids) & line_live[:, None]).astype(jnp.int32), axis=0
    )
    line_total = jnp.dot(
        newline_mask.astype(jnp.bfloat16)[None, :], newline_grad, preferred_element_type=jnp.float32
    )[0]
    kv_term = lax.dot_general(
        key_value_grad, normed, (((0,), (0,)), ((), ())), preferred_element_type=jnp.float32
    )
    kv_term = kv_term + line_total[:, None] * line_normed.astype(jnp.float32)[None, :]
    normed_grad = jnp.dot(
        key_value_grad, key_value_weight, preferred_element_type=jnp.float32
    ).astype(jnp.bfloat16)
    returning = norm_backward(recv_inverse, normed_grad.astype(jnp.float32), recv_values)
    returned = lax.all_to_all(
        returning.reshape(groups, capacity * tile_rows, share),
        "dp",
        split_axis=0,
        concat_axis=0,
        tiled=True,
    )
    tile_back = jnp.einsum(
        "gcj,gctx->jtx",
        select,
        returned.reshape(groups, capacity, tile_rows, share),
        preferred_element_type=jnp.float32,
    ).reshape(row_count, share)
    projected_grad = tile_back.astype(jnp.bfloat16)
    contract = (((0,), (0,)), ((), ()))
    siglip_term = lax.dot_general(
        siglip_features, projected_grad, contract, preferred_element_type=jnp.float32
    )
    convnext_term = lax.dot_general(
        convnext_features, projected_grad, contract, preferred_element_type=jnp.float32
    )
    siglip_result, convnext_result, kv_result = (
        lax.psum_scatter(siglip_term, "dp", scatter_dimension=0, tiled=True),
        lax.psum_scatter(convnext_term, "dp", scatter_dimension=0, tiled=True),
        lax.psum_scatter(kv_term, "dp", scatter_dimension=0, tiled=True),
    )
    return (siglip_result, convnext_result, kv_result)


FROM_X, FROM_Y, FROM_CORE, HALF_X, HALF_Y, CORE_X, CORE_Y, CORE_HX, CORE_HY = range(9)
MESH = pl.DeviceIdType.MESH


def gather_kernel(
    groups,
    sig_ref,
    conv_ref,
    sig_w_ref,
    conv_w_ref,
    kv_w_ref,
    kv_grad,
    select,
    line_part,
    line_sq,
    sig_out,
    conv_out,
    g_out,
    p_out,
    n_out,
    stats_out,
    line_out,
    f,
    g,
    proj,
    ngrad,
    sig_w,
    conv_w,
    kv_w,
    acc,
    stats,
    line_all,
    slots,
    mine,
    local_sem,
    slot_send,
    slot_recv,
    line_send,
    line_recv,
    send,
    recv,
    out_sem,
    stat_send,
    stat_recv,
    sum_send,
    sum_recv,
):
    section = lax.axis_index("section")
    z = lax.axis_index("dp")
    y = lax.axis_index("mp")
    rows, sig = sig_ref.shape
    conv = conv_ref.shape[1]
    kv = kv_grad.shape[1]
    part = rows // 8
    wide = kv // 8
    slot_rows = kv_grad.shape[0] // groups
    x_section = lax.rem(section + 2, 4)
    core_section = section + 1 - 2 * lax.rem(section, 2)
    at_x = (x_section, z, y)
    at_y = (section, z, 1 - y)
    at_core = (core_section, z, y)

    def number(sec, yy):
        return sec * 2 + yy

    me = number(section, y)
    from_x, from_y = number(x_section, y), number(section, 1 - y)
    diag = number(x_section, 1 - y)
    core = [
        number(core_section, y),
        number(lax.rem(core_section + 2, 4), y),
        number(core_section, 1 - y),
        number(lax.rem(core_section + 2, 4), 1 - y),
    ]

    def peer(k):
        return (section, lax.rem(z + k, groups), y)

    def mate(j):
        p = lax.rem(me + j, 8)
        return (lax.div(p, 2), z, lax.rem(p, 2))

    weights = [
        pltpu.make_async_copy(sig_w_ref, sig_w, local_sem.at[4]),
        pltpu.make_async_copy(conv_w_ref, conv_w, local_sem.at[5]),
        pltpu.make_async_copy(kv_w_ref, kv_w, local_sem.at[6]),
    ]

    barrier = pltpu.get_barrier_semaphore()
    for device in [peer(k) for k in range(1, groups)] + [mate(j) for j in range(1, 8)]:
        pl.semaphore_signal(barrier, inc=1, device_id=device, device_id_type=MESH)
    pl.semaphore_wait(barrier, groups + 6)

    def shard(is_f, q, m, half=None):
        if is_f:
            first, count = q * rows + m * part, part
        else:
            first, count = q * rows, rows
        if half is not None:
            count //= 2
            first = first + half * count
        first = pl.multiple_of(first, 32)
        if is_f:
            return f.at[pl.ds(first, count), :]
        return g.at[pl.ds(first, count), pl.ds(pl.multiple_of(m * wide, 128), wide)]

    def remote(ref, device, ss, rs, dst=None):
        return pltpu.make_async_remote_copy(
            src_ref=ref,
            dst_ref=ref if dst is None else dst,
            send_sem=ss,
            recv_sem=rs,
            device_id=device,
            device_id_type=MESH,
        )

    sent = []
    own = pl.ds(pl.multiple_of(z * rows, rows), rows)
    my_cols = pl.ds(pl.multiple_of(me * wide, 128), wide)

    def slot_block(q):
        return pl.ds(pl.multiple_of(q * slot_rows, slot_rows), slot_rows)

    locals_ = [
        pltpu.make_async_copy(sig_ref, f.at[own, pl.ds(0, sig)], local_sem.at[0]),
        pltpu.make_async_copy(conv_ref, f.at[own, pl.ds(sig, conv)], local_sem.at[1]),
        pltpu.make_async_copy(
            kv_grad.at[slot_block(z), my_cols], slots.at[slot_block(z), :], local_sem.at[2]
        ),
    ]
    for copy in locals_:
        copy.start()
    for k in range(1, groups):
        copy = remote(
            kv_grad.at[slot_block(lax.rem(z + k, groups)), my_cols],
            peer(k),
            slot_send.at[k],
            slot_recv.at[k],
            slots.at[slot_block(z), :],
        )
        copy.start()
        sent.append(copy)
    for k in range(1, groups):
        copy = remote(
            line_part.at[lax.rem(z + k, groups)],
            peer(k),
            sum_send.at[k],
            sum_recv.at[k],
            line_all.at[z],
        )
        copy.start()
        sent.append(copy)
    line_all[z] = line_part[z]
    for copy in locals_:
        copy.wait()

    def line(is_f):
        for k in (1, 3, 2):
            at = (0 if is_f else groups) + k
            copy = remote(shard(is_f, z, me), peer(k), line_send.at[at], line_recv.at[at])
            copy.start()
            sent.append(copy)

    line(True)
    for copy in weights:
        copy.start()
    step = 256

    def compute(is_f, q):
        block = pl.ds(pl.multiple_of(q * rows, rows), rows)

        if not is_f:
            acc[...] = jnp.zeros_like(acc)

        @pl.loop(0, proj.shape[1] // step)
        def _(n):
            cols = pl.ds(pl.multiple_of(n * step, step), step)
            if is_f:
                total = jnp.dot(
                    f[block, :sig], sig_w[:, cols], preferred_element_type=jnp.float32
                ) + jnp.dot(f[block, sig:], conv_w[:, cols], preferred_element_type=jnp.float32)
                proj[block, cols] = total.astype(jnp.bfloat16)
            else:
                total = jnp.dot(g[block, :], kv_w[:, cols], preferred_element_type=jnp.float32)
                rounded = total.astype(jnp.bfloat16)
                ngrad[block, cols] = rounded
                gv = rounded.astype(jnp.float32)
                pv = proj[block, cols].astype(jnp.float32)
                sq, pr = pv * pv, gv * pv
                acc[0] += sq[:, :128] + sq[:, 128:]
                acc[1] += pr[:, :128] + pr[:, 128:]

    def share_stats(k):
        stats[me, k, 0:1, :] = jnp.sum(acc[0].T, axis=0, keepdims=True)
        stats[me, k, 1:2, :] = jnp.sum(acc[1].T, axis=0, keepdims=True)
        stats[me, k, 2:8, :] = line_sq[2:8, :]
        for j in range(1, 8):
            copy = remote(stats.at[me, k], mate(j), stat_send.at[k, j], stat_recv.at[k, j])
            copy.start()
            sent.append(copy)

    def result(is_f, k):
        q = lax.rem(z - k + groups, groups)
        block = pl.ds(pl.multiple_of(q * rows, rows), rows)
        here, there = (proj, p_out) if is_f else (ngrad, n_out)
        at = (2 if is_f else 3) * groups + k
        copy = pltpu.make_async_copy(here.at[block, :], there.at[block, :], out_sem.at[at])
        copy.start()
        written.append(copy)

    written = []

    def put(is_f, k):
        q = lax.rem(z - k + groups, groups)
        block = pl.ds(pl.multiple_of(q * rows, rows), rows)
        if is_f:
            first = lax.div(z * (sig // groups), 128) * 128
            last = sig + z * (conv // groups)
            outs = [(f, first, sig_out, k), (f, last, conv_out, 4 * groups + k)]
        else:
            outs = [(g, z * (kv // groups), g_out, groups + k)]
        for here, column, there, at in outs:
            cols = pl.ds(pl.multiple_of(column, 128), there.shape[1])
            copy = pltpu.make_async_copy(
                here.at[block, cols], there.at[block, :], out_sem.at[at]
            )
            copy.start()
            written.append(copy)

    put(True, 0)
    for copy in weights:
        copy.wait()
    compute(True, z)
    result(True, 0)

    for k in range(1, groups):
        q = lax.rem(z - k + groups, groups)
        ref = slots.at[slot_block(q), :]
        remote(ref, peer(k), slot_send.at[k], slot_recv.at[k]).wait_recv()
    mine[...] = jnp.dot(select[...], slots[...], preferred_element_type=jnp.float32).astype(
        jnp.bfloat16
    )
    copy = pltpu.make_async_copy(mine, shard(False, z, me), local_sem.at[3])
    copy.start()
    copy.wait()
    line(False)

    items = [(False, 0), (True, 1), (True, 3), (True, 2), (False, 1), (False, 3), (False, 2)]

    def go(i, ref, device, kind):
        copy = remote(ref, device, send.at[i, kind], recv.at[i, kind])
        copy.start()
        sent.append(copy)

    def take(i, ref, kind):
        remote(ref, at_core, send.at[i, kind], recv.at[i, kind]).wait_recv()

    def owner(i):
        is_f, k = items[i]
        return is_f, lax.rem(z - k + groups, groups)

    def spread(i):
        is_f, q = owner(i)
        k = items[i][1]
        ref = shard(is_f, q, me)
        if k:
            at = (0 if is_f else groups) + k
            remote(ref, at_core, line_send.at[at], line_recv.at[at]).wait_recv()
        go(i, ref, at_x, FROM_X)
        go(i, ref, at_y, FROM_Y)
        go(i, ref, at_core, FROM_CORE)

    def forward(i):
        is_f, q = owner(i)
        take(i, shard(is_f, q, from_x), FROM_X)
        go(i, shard(is_f, q, from_x, 0), at_y, HALF_Y)
        go(i, shard(is_f, q, from_x), at_core, CORE_X)
        take(i, shard(is_f, q, from_y), FROM_Y)
        go(i, shard(is_f, q, from_y, 1), at_x, HALF_X)
        go(i, shard(is_f, q, from_y), at_core, CORE_Y)

    def halves(i):
        is_f, q = owner(i)
        take(i, shard(is_f, q, diag, 0), HALF_Y)
        go(i, shard(is_f, q, diag, 0), at_core, CORE_HY)
        take(i, shard(is_f, q, diag, 1), HALF_X)
        go(i, shard(is_f, q, diag, 1), at_core, CORE_HX)

    def finish(i):
        is_f, q = owner(i)
        take(i, shard(is_f, q, core[0]), FROM_CORE)
        take(i, shard(is_f, q, core[1]), CORE_X)
        take(i, shard(is_f, q, core[2]), CORE_Y)
        take(i, shard(is_f, q, core[3], 0), CORE_HY)
        take(i, shard(is_f, q, core[3], 1), CORE_HX)
        put(is_f, items[i][1])
        compute(is_f, q)
        if not is_f:
            share_stats(items[i][1])
        result(is_f, items[i][1])

    order = [
        (spread, 0), (spread, 1), (forward, 0), (spread, 2), (forward, 1), (halves, 0),
        (spread, 3), (forward, 2), (halves, 1), (finish, 0), (forward, 3), (halves, 2),
        (spread, 4), (finish, 1), (halves, 3), (spread, 5), (finish, 2), (forward, 4),
        (halves, 4), (spread, 6), (finish, 3), (forward, 5), (halves, 5), (forward, 6),
        (finish, 4), (halves, 6), (finish, 5), (finish, 6),
    ]
    for stage, i in order:
        stage(i)
    for k in range(1, groups):
        q = lax.rem(z - k + groups, groups)
        remote(line_all.at[q], peer(k), sum_send.at[k], sum_recv.at[k]).wait_recv()
    line_out[...] = sum([line_all[q] for q in range(1, groups)], line_all[0])
    for is_f, k in items:
        if is_f:
            continue
        for j in range(1, 8):
            ref = stats.at[lax.rem(me - j + 8, 8), k]
            remote(ref, mate(j), stat_send.at[k, j], stat_recv.at[k, j]).wait_recv()
        q = lax.rem(z - k + groups, groups)
        stats_out[:, pl.ds(pl.multiple_of(q * rows, rows), rows)] = sum(
            [stats[m, k] for m in range(1, 8)], stats[0, k]
        )
    for copy in sent:
        copy.wait_send()
    for copy in written:
        copy.wait()


def sig_window(width, groups):
    reach = max(q * width % 128 + width for q in range(groups))
    return -(-reach // 128) * 128


def gather_and_project(sig_x, conv_x, sig_w, conv_w, kv_w, kv_grad, select, line_part, line_sq):
    groups = lax.axis_size("dp")
    rows, sig = sig_x.shape
    conv = conv_x.shape[1]
    kv = kv_grad.shape[1]
    share = sig_w.shape[1]
    everything = groups * rows
    half = jnp.bfloat16
    hbm = pl.BlockSpec(memory_space=pl.ANY)
    vmem = pl.BlockSpec(memory_space=pltpu.VMEM)
    dma = pltpu.SemaphoreType.DMA
    return pl.pallas_call(
        functools.partial(gather_kernel, groups),
        out_shape=(
            jax.ShapeDtypeStruct((everything, sig_window(sig // groups, groups)), half),
            jax.ShapeDtypeStruct((everything, conv // groups), half),
            jax.ShapeDtypeStruct((everything, kv // groups), half),
            jax.ShapeDtypeStruct((everything, share), half),
            jax.ShapeDtypeStruct((everything, share), half),
            jax.ShapeDtypeStruct((8, everything), jnp.float32),
            jax.ShapeDtypeStruct((8, kv // groups), jnp.float32),
        ),
        in_specs=[hbm, hbm, hbm, hbm, hbm, hbm, vmem, vmem, vmem],
        out_specs=(hbm, hbm, hbm, hbm, hbm, vmem, vmem),
        scratch_shapes=[
            pltpu.VMEM((everything, sig + conv), half),
            pltpu.VMEM((everything, kv), half),
            pltpu.VMEM((everything, share), half),
            pltpu.VMEM((everything, share), half),
            pltpu.VMEM(sig_w.shape, half),
            pltpu.VMEM(conv_w.shape, half),
            pltpu.VMEM(kv_w.shape, half),
            pltpu.VMEM((2, rows, 128), jnp.float32),
            pltpu.VMEM((8, groups, 8, rows), jnp.float32),
            pltpu.VMEM((groups, 8, kv // groups), jnp.float32),
            pltpu.VMEM((kv_grad.shape[0], kv // 8), half),
            pltpu.VMEM((rows, kv // 8), half),
            dma((7,)),
            dma((groups,)),
            dma((groups,)),
            dma((2 * groups,)),
            dma((2 * groups,)),
            dma((2 * groups, 9)),
            dma((2 * groups, 9)),
            dma((5 * groups,)),
            dma((groups, 8)),
            dma((groups, 8)),
            dma((groups,)),
            dma((groups,)),
        ],
        compiler_params=pltpu.CompilerParams(
            collective_id=0, has_side_effects=True, vmem_limit_bytes=56 * 2**20
        ),
    )(sig_x, conv_x, sig_w, conv_w, kv_w, kv_grad, select, line_part, line_sq)


def local_gathering(
    siglip_features,
    convnext_features,
    siglip_projection,
    convnext_projection,
    newline_embed,
    key_value_weight,
    tile_rank,
    row_end,
    key_value_grad,
    newline_grad,
):
    groups = lax.axis_size("dp")
    my_rank = lax.axis_index("dp")
    dest_rank, source, slot_place = tile_places(tile_rank, groups)
    per_device = dest_rank.shape[0] // groups
    capacity = 2 * per_device // groups
    row_count, sig = siglip_features.shape
    tile_rows = row_count // per_device
    kv = key_value_grad.shape[1]

    mine_dest = lax.dynamic_slice_in_dim(dest_rank, my_rank * per_device, per_device)
    mine_place = lax.dynamic_slice_in_dim(slot_place, my_rank * per_device, per_device)
    wanted = (mine_dest * capacity + mine_place)[:, None] * tile_rows + jnp.arange(
        tile_rows, dtype=jnp.int32
    )
    select = (
        wanted.reshape(row_count, 1)
        == jnp.arange(groups * capacity * tile_rows, dtype=jnp.int32)[None, :]
    ).astype(jnp.bfloat16)
    slot_global = source * capacity + slot_place
    line_live = (dest_rank == my_rank) & (row_end == 1)
    slot_ids = jnp.arange(groups * capacity, dtype=jnp.int32)[None, :]
    newline_mask = jnp.sum(
        ((slot_global[:, None] == slot_ids) & line_live[:, None]).astype(jnp.int32), axis=0
    )
    line_total = jnp.dot(
        newline_mask.astype(jnp.bfloat16)[None, :], newline_grad, preferred_element_type=jnp.float32
    )[0]
    line_part = jnp.broadcast_to(
        line_total.reshape(groups, 1, kv // groups), (groups, 8, kv // groups)
    )
    line_vector = newline_embed.astype(jnp.float32)
    line_square = jnp.sum(line_vector * line_vector)
    sig_cols, conv_cols, grads, projected, normed_grad, stats, line_total = gather_and_project(
        siglip_features,
        convnext_features,
        siglip_projection,
        convnext_projection,
        key_value_weight,
        key_value_grad,
        select,
        line_part,
        jnp.full((8, row_count), line_square),
    )
    width = sig // groups
    sig_cols = lax.dynamic_slice_in_dim(sig_cols, lax.rem(my_rank * width, 128), width, 1)
    squares, products, line_square = stats[0], stats[1], stats[2, 0]
    line_total = line_total[0]

    proj_values = projected.astype(jnp.float32)
    grad_values = normed_grad.astype(jnp.float32)
    inverse = lax.rsqrt(squares / D + epsilon)[:, None]
    normed = (proj_values * inverse).astype(jnp.bfloat16)
    line_normed = (line_vector * lax.rsqrt(line_square / D + epsilon)).astype(jnp.bfloat16)
    projected_grad = (
        inverse * grad_values - inverse**3 * proj_values * products[:, None] / D
    ).astype(jnp.bfloat16)

    def contract(a, b):
        return lax.dot_general(a, b, (((0,), (0,)), ((), ())), preferred_element_type=jnp.float32)

    siglip_result = contract(sig_cols, projected_grad)
    convnext_result = contract(conv_cols, projected_grad)
    kv_result = contract(grads, normed)
    kv_result = kv_result + line_total[:, None] * line_normed.astype(jnp.float32)[None, :]
    return (siglip_result, convnext_result, kv_result)


GATHER_LIMIT = 40 * 2**20


def local(*args):
    rows = lax.axis_size("dp") * args[0].shape[0]
    width = args[0].shape[1] + args[1].shape[1] + args[8].shape[1]
    plane = (lax.axis_size("section"), lax.axis_size("dp"), lax.axis_size("mp"))
    if 2 * rows * width <= GATHER_LIMIT and plane == (4, 4, 2):
        return local_gathering(*args)
    return local_reducing(*args)


def solution(mesh):
    in_specs = (
        P("dp", None),
        P("dp", None),
        P(None, ("section", "mp")),
        P(None, ("section", "mp")),
        P(("section", "mp")),
        P(None, ("section", "mp")),
        P(),
        P(),
        P("dp", None),
        P("dp", None),
    )
    out_specs = (P("dp", ("section", "mp")), P("dp", ("section", "mp")), P("dp", ("section", "mp")))
    return jax.shard_map(local, mesh=mesh, in_specs=in_specs, out_specs=out_specs, check_vma=False)
```
